128 devices in a mesh: row: 16 (over z_hi, y, core), col: 8 (over z_lo, x).
Axes of the slice: x: 4, y: 4, z: 4 (z_hi: 2, z_lo: 2; z = z_hi * 2 + z_lo), core: 2. Of those that a mesh axis runs over, the one named last changes fastest.
Arguments:
- blocks: bfloat16 [512, 1024, 128], P('row', 'col'), may hold values from -6 to 6
- block_atom: int32 [512, 8], P('row', 'col'), may hold values from 0 to 63, as said below
- block_col: int32 [512, 8], P('row', 'col'), may hold values from 0 to 7
- block_count: int32 [16, 8], P('row', 'col'), may hold values from 0 to 32, as said below
Outputs:
- sign_step: float32 [8192, 8192], P('row', 'col')
The draws below stay inside these ranges and needn't reach their ends.
Inputs may be any that keep to these rules, and one draw needn't show every extreme that they name: Entries from block_count on are padding. `block_atom`: used entries of one grid column name distinct blocks; one owner's list names at most 2 blocks of the block rows of any one grid row.
All inputs are finite; a program needn't handle non-finite values.
Results may differ from the reference program's by a relative error of at most 0.0045.
Values may be sent and summed in bfloat16 or wider, within the bound.
No kernel may reach another device: no remote copies, remote signals or barrier semaphores. Data moves between devices by JAX's collectives and lax.ppermute only.
A program may use at most 128 MiB of HBM per device.

```python
import jax
import jax.numpy as jnp
from jax import lax

BLOCK = 128
BR = 4
CAP = 2
NB = 64
BC = 8
SLOTS = 32
N_ROW = 16
N_COL = 8


def column_layout(key):
    row_count = NB // BR
    tile_size = BR * BC
    k_heavy, k_count, k_order, k_place, k_slot = jax.random.split(key, 5)
    heavy_owner = jax.random.randint(k_heavy, (), 0, row_count)
    owners = jnp.arange(row_count, dtype=jnp.int32)
    counts = jax.random.randint(k_count, (row_count, row_count), 0, CAP + 1)
    counts = jnp.where(owners[None, :] == heavy_owner, CAP, counts)

    def owner_perm(subkey):
        return jax.random.permutation(subkey, row_count).astype(jnp.int32)
    owner_ranks = jax.vmap(owner_perm)(jax.random.split(k_order, row_count))
    sort_score = jnp.where(owners[None, :] == heavy_owner, -1, owner_ranks)
    owner_order = jnp.argsort(sort_score, axis=1)
    ordered = jnp.take_along_axis(counts, owner_order, 1)
    run_ends = jnp.cumsum(ordered, axis=1)
    begins = run_ends - ordered
    kept_count = jnp.clip(tile_size - begins, 0, ordered)
    inverse = jnp.argsort(owner_order, axis=1)
    kept_owner = jnp.take_along_axis(kept_count, inverse, 1)
    begin_owner = jnp.take_along_axis(begins, inverse, 1)

    def place_perm(subkey):
        return jax.random.permutation(subkey, tile_size).astype(jnp.int32)
    places = jax.vmap(place_perm)(jax.random.split(k_place, row_count))
    turn_index = jnp.arange(CAP, dtype=jnp.int32)
    slot_index = jnp.minimum(begin_owner[:, :, None] + turn_index[None, None, :], tile_size - 1)
    target_rows = jnp.arange(row_count, dtype=jnp.int32)[:, None, None]
    position = places[target_rows, slot_index]
    is_live = turn_index[None, None, :] < kept_owner[:, :, None]
    atom_ids = target_rows * BR + position // BC
    column_ids = position % BC
    atom_ids = atom_ids.transpose(1, 0, 2).reshape(row_count, SLOTS)
    column_ids = column_ids.transpose(1, 0, 2).reshape(row_count, SLOTS)
    is_live = is_live.transpose(1, 0, 2).reshape(row_count, SLOTS)

    def slot_perm(subkey):
        return jax.random.permutation(subkey, SLOTS).astype(jnp.int32)
    slot_ranks = jax.vmap(slot_perm)(jax.random.split(k_slot, row_count))
    chosen = jnp.argsort(jnp.where(is_live, 0, SLOTS) + slot_ranks, axis=1)
    atom_ids = jnp.take_along_axis(atom_ids, chosen, 1)
    column_ids = jnp.take_along_axis(column_ids, chosen, 1)
    is_live = jnp.take_along_axis(is_live, chosen, 1)
    used_count = jnp.sum(is_live.astype(jnp.int32), axis=1)
    return (atom_ids, column_ids, is_live, used_count)


def whole_layout(key):
    column_total = NB // BC
    keys = jax.random.split(key, column_total)
    atom_ids, column_ids, is_live, used_count = jax.vmap(column_layout)(keys)
    row_count = NB // BR
    atom_ids = atom_ids.transpose(1, 2, 0).reshape(row_count * SLOTS, column_total)
    column_ids = column_ids.transpose(1, 2, 0).reshape(row_count * SLOTS, column_total)
    is_live = is_live.transpose(1, 2, 0).reshape(row_count * SLOTS, column_total)
    return (atom_ids, column_ids, is_live, used_count.T)


def draw_block_atom(key, part):
    atom_ids, column_ids, is_live, used_count = whole_layout(key)
    key = jax.random.fold_in(key, 11)
    filler = jax.random.randint(key, atom_ids.shape, 0, NB)
    return jnp.where(is_live, atom_ids, filler).astype(jnp.int32)


def draw_block_col(key, part):
    atom_ids, column_ids, is_live, used_count = whole_layout(key)
    key = jax.random.fold_in(key, 23)
    filler = jax.random.randint(key, column_ids.shape, 0, BC)
    return jnp.where(is_live, column_ids, filler).astype(jnp.int32)


def draw_block_count(key, part):
    atom_ids, column_ids, is_live, used_count = whole_layout(key)
    return used_count.astype(jnp.int32)


def steps_of(key, shape, shards, low, high):
    gain, own = 1.0, jax.random.fold_in(key, 6)
    for dim, shards_of in shards:
        draws = jnp.exp(jax.random.uniform(jax.random.fold_in(own, dim), (shards_of,), jnp.float32, low / len(shards), high / len(shards)))
        gain = gain * jnp.repeat(draws, shape[dim] // shards_of).reshape([-1 if axis == dim else 1 for axis in range(len(shape))])
    return gain


def normal_values(key, dims, spread, reach, shards=(), kind=jnp.bfloat16):
    entries = jax.random.normal(key, dims, jnp.float32) * spread
    if len(shards) > 0:
        entries = steps_of(key, dims, shards, -0.22, 0.18) * entries
    return jnp.clip(entries, min=-reach, max=reach).astype(kind)


def setup_inputs(seed: int = 0) -> dict:
    seeds = jax.random.split(jax.random.key(seed), 5)
    blocks = normal_values(seeds[0], (N_ROW * SLOTS, N_COL * BLOCK, BLOCK), 1.0, 6.0, ((0, 16), (1, 8)))
    block_atom = draw_block_atom(jax.random.fold_in(seeds[4], 71), 0)
    block_col = draw_block_col(jax.random.fold_in(seeds[4], 71), 0)
    block_count = draw_block_count(jax.random.fold_in(seeds[4], 71), 0)
    return dict(blocks=blocks, block_atom=block_atom, block_col=block_col, block_count=block_count)


def reference(blocks, block_atom, block_col, block_count):
    values = blocks.reshape(N_ROW, SLOTS, N_COL, BLOCK, BLOCK)
    atom_ids = block_atom.reshape(N_ROW, SLOTS, N_COL)
    column_ids = block_col.reshape(N_ROW, SLOTS, N_COL)
    is_used = jnp.arange(SLOTS, dtype=jnp.int32)[None, :, None] < block_count[:, None, :]
    row_target = jnp.where(is_used, atom_ids, NB).astype(jnp.int32)
    column_target = (jnp.arange(N_COL, dtype=jnp.int32)[None, None, :] * BC + column_ids).astype(jnp.int32)
    block_grid = jnp.zeros((NB, NB, BLOCK, BLOCK), blocks.dtype)
    block_grid = block_grid.at[row_target, column_target].set(values, mode="drop")
    dense_matrix = block_grid.transpose(0, 2, 1, 3).reshape(NB * BLOCK, NB * BLOCK)
    wide_matrix = dense_matrix.astype(jnp.float32)
    square = jnp.dot(wide_matrix, wide_matrix, precision=lax.Precision.HIGHEST)
    half_square = (square * (0.5 / (NB * BLOCK))).astype(jnp.bfloat16)
    product = jnp.dot(wide_matrix, half_square.astype(jnp.float32), precision=lax.Precision.HIGHEST)
    return 1.5 * wide_matrix - product
```

```python
import functools

import jax
import jax.numpy as jnp
from jax import lax
from jax.experimental import pallas as pl
from jax.experimental.pallas import tpu as pltpu
from jax.sharding import PartitionSpec as P

BLOCK = 128
BR = 4
BC = 8
CAP = 2
META = 16
NONE = 64


def pack_kernel(atom, column, count, blocks, send, seen, place):
    groups = send.shape[0]
    slots = blocks.shape[0]
    send[...] = jnp.zeros_like(send)
    for group in range(groups):
        seen[group] = 0
        for turn in range(CAP):
            place[group * CAP + turn] = NONE

    @pl.loop(0, slots)
    def _(slot):
        @pl.when(slot < count[0, 0])
        def _():
            group = atom[slot] // BR
            turn = jnp.minimum(seen[group], CAP - 1)
            seen[group] = turn + 1
            place[group * CAP + turn] = atom[slot] % BR * BC + column[slot]
            start = pl.multiple_of(turn * BLOCK, BLOCK)
            send[group, pl.ds(start, BLOCK), :] = blocks[slot]

    row = lax.broadcasted_iota(jnp.int32, (META, BLOCK), 0)
    for group in range(groups):
        value = jnp.where(row == 0, place[group * CAP], place[group * CAP + 1])
        send[group, CAP * BLOCK :, :] = value.astype(jnp.float32).astype(send.dtype)


def unpack_kernel(received, tile, place_vector, place, sem):
    owners = received.shape[0]
    tile[...] = jnp.zeros_like(tile)
    lane = lax.broadcasted_iota(jnp.int32, (META, BLOCK), 1)
    places = jnp.full((META, BLOCK), NONE, jnp.int32)
    for owner in range(owners):
        value = received[owner, CAP * BLOCK :, :].astype(jnp.float32).astype(jnp.int32)
        places = jnp.where(lane == owner, value, places)
    place_vector[...] = places
    copy = pltpu.make_async_copy(place_vector, place, sem)
    copy.start()
    copy.wait()

    @pl.loop(0, owners)
    def _(owner):
        for turn in range(CAP):
            at = place[turn, owner]

            @pl.when(at < BR * BC)
            def _():
                top = pl.multiple_of(at // BC * BLOCK, BLOCK)
                left = pl.multiple_of(at % BC * BLOCK, BLOCK)
                block = received[owner, turn * BLOCK : (turn + 1) * BLOCK, :]
                tile[pl.ds(top, BLOCK), pl.ds(left, BLOCK)] = block


def local_tile(blocks, block_atom, block_col, block_count):
    owners = lax.axis_size("row")
    vmem = pl.BlockSpec(memory_space=pltpu.VMEM)
    smem = pl.BlockSpec(memory_space=pltpu.SMEM)
    send = pl.pallas_call(
        pack_kernel,
        out_shape=jax.ShapeDtypeStruct((owners, CAP * BLOCK + META, BLOCK), blocks.dtype),
        in_specs=[smem, smem, smem, vmem],
        out_specs=vmem,
        scratch_shapes=[pltpu.SMEM((owners,), jnp.int32), pltpu.SMEM((owners * CAP,), jnp.int32)],
        compiler_params=pltpu.CompilerParams(vmem_limit_bytes=16 << 20),
        name="pack",
    )(block_atom[:, 0], block_col[:, 0], block_count, blocks)
    received = lax.all_to_all(send, "row", 0, 0, tiled=True)
    return pl.pallas_call(
        unpack_kernel,
        out_shape=jax.ShapeDtypeStruct((BR * BLOCK, BC * BLOCK), blocks.dtype),
        in_specs=[vmem],
        out_specs=vmem,
        scratch_shapes=[
            pltpu.VMEM((META, BLOCK), jnp.int32),
            pltpu.SMEM((META, BLOCK), jnp.int32),
            pltpu.SemaphoreType.DMA,
        ],
        compiler_params=pltpu.CompilerParams(vmem_limit_bytes=16 << 20),
        name="unpack",
    )(received)


def local(blocks, block_atom, block_col, block_count):
    matrix = local_tile(blocks, block_atom, block_col, block_count)
    row_strip = lax.all_gather(matrix, "col", axis=1, tiled=True)
    column_strip = lax.all_gather(matrix, "row", axis=0, tiled=True)
    factor = 0.5 / row_strip.shape[1]
    square = jnp.dot(row_strip, column_strip, preferred_element_type=jnp.float32)
    half_square = (square * factor).astype(jnp.bfloat16)
    half_strip = lax.all_gather(half_square, "col", axis=1, tiled=True)
    product = jnp.dot(half_strip, column_strip, preferred_element_type=jnp.float32)
    return 1.5 * matrix.astype(jnp.float32) - product


def solution(mesh):
    placed = (P("row", "col", None), P("row", "col"), P("row", "col"), P("row", "col"))
    return jax.shard_map(
        local, mesh=mesh, in_specs=placed, out_specs=P("row", "col"), check_vma=False
    )
```

```python
import functools

import jax
import jax.numpy as jnp
from jax import lax
from jax.experimental import pallas as pl
from jax.experimental.pallas import tpu as pltpu
from jax.sharding import PartitionSpec as P

BLOCK = 128
BR = 4
BC = 8
CAP = 2
META = 16
NONE = 64


def pack_kernel(atom, column, count, blocks, send, seen, place):
    groups = send.shape[0]
    slots = blocks.shape[0]
    send[...] = jnp.zeros_like(send)
    for group in range(groups):
        seen[group] = 0
        for turn in range(CAP):
            place[group * CAP + turn] = NONE

    @pl.loop(0, slots)
    def _(slot):
        @pl.when(slot < count[0, 0])
        def _():
            group = atom[slot] // BR
            turn = jnp.minimum(seen[group], CAP - 1)
            seen[group] = turn + 1
            place[group * CAP + turn] = atom[slot] % BR * BC + column[slot]
            start = pl.multiple_of(turn * BLOCK, BLOCK)
            send[group, pl.ds(start, BLOCK), :] = blocks[slot]

    row = lax.broadcasted_iota(jnp.int32, (META, BLOCK), 0)
    for group in range(groups):
        value = jnp.where(row == 0, place[group * CAP], place[group * CAP + 1])
        send[group, CAP * BLOCK :, :] = value.astype(jnp.float32).astype(send.dtype)


def unpack_kernel(received, tile, place_vector, place, sem):
    owners = received.shape[0]
    tile[...] = jnp.zeros_like(tile)
    lane = lax.broadcasted_iota(jnp.int32, (META, BLOCK), 1)
    places = jnp.full((META, BLOCK), NONE, jnp.int32)
    for owner in range(owners):
        value = received[owner, CAP * BLOCK :, :].astype(jnp.float32).astype(jnp.int32)
        places = jnp.where(lane == owner, value, places)
    place_vector[...] = places
    copy = pltpu.make_async_copy(place_vector, place, sem)
    copy.start()
    copy.wait()

    @pl.loop(0, owners)
    def _(owner):
        for turn in range(CAP):
            at = place[turn, owner]

            @pl.when(at < BR * BC)
            def _():
                top = pl.multiple_of(at // BC * BLOCK, BLOCK)
                left = pl.multiple_of(at % BC * BLOCK, BLOCK)
                block = received[owner, turn * BLOCK : (turn + 1) * BLOCK, :]
                tile[pl.ds(top, BLOCK), pl.ds(left, BLOCK)] = block


def local_tile(blocks, block_atom, block_col, block_count):
    owners = lax.axis_size("row")
    vmem = pl.BlockSpec(memory_space=pltpu.VMEM)
    smem = pl.BlockSpec(memory_space=pltpu.SMEM)
    send = pl.pallas_call(
        pack_kernel,
        out_shape=jax.ShapeDtypeStruct((owners, CAP * BLOCK + META, BLOCK), blocks.dtype),
        in_specs=[smem, smem, smem, vmem],
        out_specs=vmem,
        scratch_shapes=[pltpu.SMEM((owners,), jnp.int32), pltpu.SMEM((owners * CAP,), jnp.int32)],
        compiler_params=pltpu.CompilerParams(vmem_limit_bytes=16 << 20),
        name="pack",
    )(block_atom[:, 0], block_col[:, 0], block_count, blocks)
    received = lax.all_to_all(send, "row", 0, 0, tiled=True)
    return pl.pallas_call(
        unpack_kernel,
        out_shape=jax.ShapeDtypeStruct((BR * BLOCK, BC * BLOCK), blocks.dtype),
        in_specs=[vmem],
        out_specs=vmem,
        scratch_shapes=[
            pltpu.VMEM((META, BLOCK), jnp.int32),
            pltpu.SMEM((META, BLOCK), jnp.int32),
            pltpu.SemaphoreType.DMA,
        ],
        compiler_params=pltpu.CompilerParams(vmem_limit_bytes=16 << 20),
        name="unpack",
    )(received)


def product_kernel(factor, left_parts, right_rows, first_row, has_base, left_at, right_at, *refs):
    lefts, refs = refs[: len(left_parts)], refs[len(left_parts) :]
    pieces_total = sum(map(len, right_rows))
    rights, refs = refs[:pieces_total], refs[pieces_total:]
    if has_base:
        base, refs = refs[0], refs[1:]
    out, held, staged, total, left_sems, right_sems = refs
    depth = staged.shape[1]
    copies = []
    for index, (left, (source, first, count)) in enumerate(zip(lefts, left_parts)):
        for side in range(2):
            copy = pltpu.make_async_copy(
                left.at[pl.ds(source, count), pl.ds(side * depth, depth)],
                held.at[left_at[index] * 2 + side, pl.ds(first, count)],
                left_sems.at[index, side],
            )
            copy.start()
            copies.append(copy)
    slots = staged.shape[0]
    loads, at = [], 0
    for index, pieces in enumerate(right_rows):
        load = []
        for part, (first, count) in enumerate(pieces):
            load.append(
                pltpu.make_async_copy(
                    rights[at],
                    staged.at[index % slots, pl.ds(first, count)],
                    right_sems.at[index % slots, part],
                )
            )
            at += 1
        loads.append(load)
    for load in loads[: slots - 1]:
        for copy in load:
            copy.start()
    for copy in copies:
        copy.wait()
    for index in range(len(loads)):
        ahead = index + slots - 1
        if ahead < len(loads):
            for copy in loads[ahead]:
                copy.start()
        for copy in loads[index]:
            copy.wait()
        term = jnp.dot(
            held[right_at[index]], staged[index % slots], preferred_element_type=jnp.float32
        )
        if index == 0:
            total[...] = term
        elif index < len(loads) - 1:
            total[...] += term
        else:
            value = (total[...] + term) * factor
            if has_base:
                value = 1.5 * base[...].astype(jnp.float32) - value
            out[...] = value.astype(out.dtype)


def product(lefts, rights, rows, factor, dtype, name, base=None):
    width = lefts[0][0].shape[1]
    right_arrays = [array for _, pieces in rights for array, _ in pieces]
    columns = right_arrays[0].shape[1]
    depth = width // 2
    left_parts = [(source, first, count) for _, _, source, first, count in lefts]
    right_rows = [[(first, array.shape[0]) for array, first in pieces] for _, pieces in rights]
    left_at = jnp.stack([part[1] for part in lefts]).astype(jnp.int32)
    right_at = jnp.stack([chunk for chunk, _ in rights]).astype(jnp.int32)
    smem = pl.BlockSpec(memory_space=pltpu.SMEM)
    vmem = pl.BlockSpec(memory_space=pltpu.VMEM)
    hbm = pl.BlockSpec(memory_space=pltpu.HBM)
    operands = [left_at, right_at] + [part[0] for part in lefts] + right_arrays
    specs = [smem, smem] + [hbm] * (len(operands) - 2)
    if base is not None:
        operands.append(base)
        specs.append(vmem)
    slots = 4
    return pl.pallas_call(
        functools.partial(product_kernel, factor, left_parts, right_rows, 0, base is not None),
        out_shape=jax.ShapeDtypeStruct((rows, columns), dtype),
        in_specs=specs,
        out_specs=vmem,
        scratch_shapes=[
            pltpu.VMEM((len(rights), rows, depth), lefts[0][0].dtype),
            pltpu.VMEM((slots, depth, columns), lefts[0][0].dtype),
            pltpu.VMEM((rows, columns), jnp.float32),
            pltpu.SemaphoreType.DMA((len(lefts), 2)),
            pltpu.SemaphoreType.DMA((slots, 2)),
        ],
        compiler_params=pltpu.CompilerParams(vmem_limit_bytes=48 << 20),
        cost_estimate=pl.CostEstimate(
            flops=2 * rows * columns * depth * len(rights),
            bytes_accessed=2 * depth * len(rights) * (rows + columns),
            transcendentals=0,
        ),
        name=name,
    )(*operands)


def over_row(value, z_step, y_step, core_step):
    size = lax.axis_size("row")
    pairs = []
    for source in range(size):
        z, y, core = source // 8, source // 2 % 4, source % 2
        target = ((z + z_step) % 2 * 4 + (y + y_step) % 4) * 2 + (core + core_step) % 2
        pairs.append((source, target))
    return lax.ppermute(value, "row", pairs)


def over_col(value, z_step, x_step):
    size = lax.axis_size("col")
    pairs = []
    for source in range(size):
        z, x = source // 4, source % 4
        pairs.append((source, (z + z_step) % 2 * 4 + (x + x_step) % 4))
    return lax.ppermute(value, "col", pairs)


def x_shift(value, step):
    return over_col(value, 0, step)


def y_shift(value, step):
    return over_row(value, 0, step, 0)


def z_swap(value):
    return over_col(value, 1, 0)


def core_swap(value):
    return over_row(value, 0, 0, 1)


def after(values, *earlier):
    return lax.optimization_barrier((values, earlier))[0]


def near(value, shift):
    return shift(value, 1), shift(value, -1)


def far(below, above, shift):
    half = below.shape[0] // 2
    return shift(below[:half], 1), shift(above[half:], -1)


def local(blocks, block_atom, block_col, block_count):
    matrix = local_tile(blocks, block_atom, block_col, block_count)
    rows = matrix.shape[0]
    half = rows // 2
    quarter = half // 2
    row, col = lax.axis_index("row"), lax.axis_index("col")
    z_hi, y, core = row // 8, row // 2 % 4, row % 2
    z_lo, x = col // 4, col % 4

    def col_chunk(z_step, x_step):
        return (z_lo + z_step) % 2 * 4 + (x + x_step) % 4

    def row_chunk(z_step, y_step, core_step):
        return ((z_hi + z_step) % 2 * 4 + (y + y_step) % 4) * 2 + (core + core_step) % 2

    top, bottom = matrix[:half], matrix[half:]
    other_z = over_row(matrix, 1, 0, 0)
    x_near = near(matrix, x_shift)
    y_near = near(matrix, y_shift)
    top, bottom, matrix_b, other_z, x_near, y_near = after((top, bottom, matrix, other_z, x_near, y_near))
    top_z = z_swap(top)
    x_far = far(*x_near, x_shift)
    y_far = far(*y_near, y_shift)
    z_near = near(other_z, y_shift)
    swapped = {}
    swapped["own"] = core_swap(matrix_b)
    swapped["near"] = [core_swap(v) for v in y_near]
    bottom, top_z, x_far = after((bottom, top_z, x_far))
    bottom_z = z_swap(bottom)
    top_z_near = near(top_z, x_shift)
    bottom_z, top_z_near = after((bottom_z, top_z_near))
    top_z_far = far(*top_z_near, x_shift)
    bottom_z_near = near(bottom_z, x_shift)
    z_near, y_far, top_z_far, other_z_b = after((z_near, y_far, top_z_far, other_z))
    z_far = far(*z_near, y_shift)
    swapped["far"] = [core_swap(v) for v in y_far]
    swapped["z"] = core_swap(other_z_b)
    swapped["z near"] = [core_swap(v) for v in z_near]
    bottom_z_near, z_far_b = after((bottom_z_near, z_far))
    bottom_z_far = far(*bottom_z_near, x_shift)
    z_far = z_far_b
    swapped["z far"] = [core_swap(v) for v in z_far]

    pieces = [
        (0, 0, [(matrix, 0)], [(swapped["own"], 0)]),
        (0, -1, [(y_near[0], 0)], [(swapped["near"][0], 0)]),
        (0, 1, [(y_near[1], 0)], [(swapped["near"][1], 0)]),
        (0, 2, [(y_far[0], 0), (y_far[1], half)], [(swapped["far"][0], 0), (swapped["far"][1], half)]),
        (1, 0, [(other_z, 0)], [(swapped["z"], 0)]),
        (1, -1, [(z_near[0], 0)], [(swapped["z near"][0], 0)]),
        (1, 1, [(z_near[1], 0)], [(swapped["z near"][1], 0)]),
        (1, 2, [(z_far[0], 0), (z_far[1], half)], [(swapped["z far"][0], 0), (swapped["z far"][1], half)]),
    ]
    chunks = []
    for z_step, y_step, mine, others in pieces:
        chunks.append((row_chunk(z_step, y_step, 0), mine))
        chunks.append((row_chunk(z_step, y_step, 1), others))

    def strip(z_step, own, near_two, far_two, source=0):
        return [
            (own, col_chunk(z_step, 0), source, 0, half),
            (near_two[0], col_chunk(z_step, -1), source, 0, half),
            (near_two[1], col_chunk(z_step, 1), source, 0, half),
            (far_two[0], col_chunk(z_step, 2), 0, 0, quarter),
            (far_two[1], col_chunk(z_step, 2), 0, quarter, quarter),
        ]

    def own_strip(source, far_one):
        return strip(0, matrix, x_near, x_far, source)[:3] + [(far_one, col_chunk(0, 2), 0, 0, half)]

    factor = 0.5 / (matrix.shape[1] * lax.axis_size("col"))
    kind = matrix.dtype
    lefts = own_strip(0, x_far[0]) + strip(1, top_z, top_z_near, top_z_far)
    half_top = product(lefts, chunks, half, factor, kind, "square_top")
    top_near = near(half_top, x_shift)
    top_swapped = z_swap(half_top)
    bottom_z, bottom_z_near, bottom_z_far = after((bottom_z, bottom_z_near, bottom_z_far), half_top)
    lefts = own_strip(half, x_far[1]) + strip(1, bottom_z, bottom_z_near, bottom_z_far)
    half_bottom = product(lefts, chunks, half, factor, kind, "square_bottom")
    bottom_swapped = z_swap(half_bottom)
    bottom_near = near(half_bottom, x_shift)
    top_near, half_bottom = after((top_near, half_bottom))
    top_far = far(*top_near, x_shift)
    top_swapped_near = [z_swap(v) for v in top_near]
    bottom_near, bottom_swapped, top_far, top_swapped = after((bottom_near, bottom_swapped, top_far, top_swapped))
    bottom_far = far(*bottom_near, x_shift)
    bottom_swapped_near = near(bottom_swapped, x_shift)
    top_swapped_far = [z_swap(v) for v in top_far]
    bottom_swapped_near = after(bottom_swapped_near, bottom_far)
    bottom_swapped_far = far(*bottom_swapped_near, x_shift)
    lefts = strip(0, half_top, top_near, top_far) + strip(1, top_swapped, top_swapped_near, top_swapped_far)
    out_top = product(lefts, chunks, half, 1.0, jnp.float32, "step_top", top)
    lefts = strip(0, half_bottom, bottom_near, bottom_far)
    lefts += strip(1, bottom_swapped, bottom_swapped_near, bottom_swapped_far)
    out_bottom = product(lefts, chunks, half, 1.0, jnp.float32, "step_bottom", matrix[half:])
    return jnp.concatenate([out_top, out_bottom], axis=0)


def solution(mesh):
    placed = (P("row", "col", None), P("row", "col"), P("row", "col"), P("row", "col"))
    return jax.shard_map(
        local, mesh=mesh, in_specs=placed, out_specs=P("row", "col"), check_vma=False
    )
```

```python
import functools

import jax
import jax.numpy as jnp
from jax import lax
from jax.experimental import pallas as pl
from jax.experimental.pallas import tpu as pltpu
from jax.sharding import PartitionSpec as P

BLOCK = 128
BR = 4
BC = 8
CAP = 2
META = 16
NONE = 64


def pack_kernel(atom, column, count, blocks, send, seen, place):
    groups = send.shape[0]
    slots = blocks.shape[0]
    send[...] = jnp.zeros_like(send)
    for group in range(groups):
        seen[group] = 0
        for turn in range(CAP):
            place[group * CAP + turn] = NONE

    @pl.loop(0, slots)
    def _(slot):
        @pl.when(slot < count[0, 0])
        def _():
            group = atom[slot] // BR
            turn = jnp.minimum(seen[group], CAP - 1)
            seen[group] = turn + 1
            place[group * CAP + turn] = atom[slot] % BR * BC + column[slot]
            start = pl.multiple_of(turn * BLOCK, BLOCK)
            send[group, pl.ds(start, BLOCK), :] = blocks[slot]

    row = lax.broadcasted_iota(jnp.int32, (META, BLOCK), 0)
    for group in range(groups):
        value = jnp.where(row == 0, place[group * CAP], place[group * CAP + 1])
        send[group, CAP * BLOCK :, :] = value.astype(jnp.float32).astype(send.dtype)


def unpack_kernel(received, tile, place_vector, place, sem):
    owners = received.shape[0]
    tile[...] = jnp.zeros_like(tile)
    lane = lax.broadcasted_iota(jnp.int32, (META, BLOCK), 1)
    places = jnp.full((META, BLOCK), NONE, jnp.int32)
    for owner in range(owners):
        value = received[owner, CAP * BLOCK :, :].astype(jnp.float32).astype(jnp.int32)
        places = jnp.where(lane == owner, value, places)
    place_vector[...] = places
    copy = pltpu.make_async_copy(place_vector, place, sem)
    copy.start()
    copy.wait()

    @pl.loop(0, owners)
    def _(owner):
        for turn in range(CAP):
            at = place[turn, owner]

            @pl.when(at < BR * BC)
            def _():
                top = pl.multiple_of(at // BC * BLOCK, BLOCK)
                left = pl.multiple_of(at % BC * BLOCK, BLOCK)
                block = received[owner, turn * BLOCK : (turn + 1) * BLOCK, :]
                tile[pl.ds(top, BLOCK), pl.ds(left, BLOCK)] = block


def local_tile(blocks, block_atom, block_col, block_count):
    owners = lax.axis_size("row")
    vmem = pl.BlockSpec(memory_space=pltpu.VMEM)
    smem = pl.BlockSpec(memory_space=pltpu.SMEM)
    send = pl.pallas_call(
        pack_kernel,
        out_shape=jax.ShapeDtypeStruct((owners, CAP * BLOCK + META, BLOCK), blocks.dtype),
        in_specs=[smem, smem, smem, vmem],
        out_specs=vmem,
        scratch_shapes=[pltpu.SMEM((owners,), jnp.int32), pltpu.SMEM((owners * CAP,), jnp.int32)],
        compiler_params=pltpu.CompilerParams(vmem_limit_bytes=16 << 20),
        name="pack",
    )(block_atom[:, 0], block_col[:, 0], block_count, blocks)
    received = lax.all_to_all(send, "row", 0, 0, tiled=True)
    return pl.pallas_call(
        unpack_kernel,
        out_shape=jax.ShapeDtypeStruct((BR * BLOCK, BC * BLOCK), blocks.dtype),
        in_specs=[vmem],
        out_specs=vmem,
        scratch_shapes=[
            pltpu.VMEM((META, BLOCK), jnp.int32),
            pltpu.SMEM((META, BLOCK), jnp.int32),
            pltpu.SemaphoreType.DMA,
        ],
        compiler_params=pltpu.CompilerParams(vmem_limit_bytes=16 << 20),
        name="unpack",
    )(received)


def product_kernel(factor, left_parts, right_parts, part, first_total, has_base, n_out, left_at, right_at, core, want, *refs):
    lefts, refs = refs[: len(left_parts)], refs[len(left_parts) :]
    n_right = sum(len(pieces) for chunk in right_parts for pieces in chunk)
    rights, refs = list(refs[:n_right]), refs[n_right:]
    if first_total:
        total_in, refs = refs[0], refs[1:]
    if has_base:
        base, refs = refs[0], refs[1:]
    outs, (held, staged, total, left_sems, right_sems) = refs[:n_out], refs[n_out:]
    places, (slots, depth, _) = held.shape[0], staged.shape
    copies = []
    for index, (left, (source, first, count)) in enumerate(zip(lefts, left_parts)):
        target = held.at[left_at[index] % places, pl.ds(first, count)]
        copies.append(pltpu.make_async_copy(left.at[pl.ds(source, count)], target, left_sems.at[index]))
    loads = []
    for index, chunk in enumerate(right_parts):
        load = []
        for step, pieces in enumerate(chunk):
            down = (core[0] + step) % 2 * (depth // 2)
            for first, count in pieces:
                target = staged.at[index % slots, pl.ds(pl.multiple_of(down + first, count), count)]
                sem = right_sems.at[index % slots, len(load)]
                load.append(pltpu.make_async_copy(rights.pop(0), target, sem))
        loads.append(load)

    def when_wanted(index, act):
        if part:
            pl.when(right_at[index] // places == want[0])(act)
        else:
            act()

    def start(index):
        for load in loads[index]:
            load.start()

    for copy in copies:
        copy.start()
    when_wanted(0, functools.partial(start, 0))
    total[...] = total_in[...] if first_total else jnp.zeros_like(total)
    for copy in copies:
        copy.wait()
    for index in range(1, slots - 1):
        when_wanted(index, functools.partial(start, index))
    for index in range(len(loads)):
        ahead = index + slots - 1
        if ahead < len(loads):
            when_wanted(ahead, functools.partial(start, ahead))

        def add():
            for load in loads[index]:
                load.wait()
            left = held[right_at[index] % places]
            total[...] += jnp.dot(left, staged[index % slots], preferred_element_type=jnp.float32)

        when_wanted(index, add)
    first = 0
    for out in outs:
        count = out.shape[0]
        value = total[first : first + count, :] * factor
        if has_base:
            value = 1.5 * base[first : first + count, :].astype(jnp.float32) - value
        out[...] = value.astype(out.dtype)
        first += count


def product(lefts, rights, core, outs, factor, dtype, name, part=None, first_total=None, base=None):
    width = lefts[0][0].shape[1]
    kind = lefts[0][0].dtype
    left_parts = [(source, first, count) for _, _, source, first, count in lefts]
    right_parts = [
        [[(first, array.shape[0]) for array, first in pieces] for pieces in chunk[1:]] for chunk in rights
    ]
    left_at = jnp.stack([chunk for _, chunk, *_ in lefts]).astype(jnp.int32)
    right_at = jnp.stack([chunk for chunk, *_ in rights]).astype(jnp.int32)
    want = jnp.asarray(0 if part is None else part, jnp.int32)[None]
    smem = pl.BlockSpec(memory_space=pltpu.SMEM)
    vmem = pl.BlockSpec(memory_space=pltpu.VMEM)
    hbm = pl.BlockSpec(memory_space=pltpu.HBM)
    arrays = [left for left, *_ in lefts]
    arrays += [array for chunk in rights for pieces in chunk[1:] for array, _ in pieces]
    extra = [value for value in (first_total, base) if value is not None]
    count = len(rights) if part is None else len(rights) // 2
    rows = sum(outs)
    slots = 3
    return pl.pallas_call(
        functools.partial(
            product_kernel,
            factor,
            left_parts,
            right_parts,
            part is not None,
            first_total is not None,
            base is not None,
            len(outs),
        ),
        out_shape=[jax.ShapeDtypeStruct((out, width), dtype) for out in outs],
        in_specs=[smem] * 4 + [hbm] * len(arrays) + [vmem] * len(extra),
        out_specs=[vmem] * len(outs),
        scratch_shapes=[
            pltpu.VMEM((count, rows, width), kind),
            pltpu.VMEM((slots, width, width), kind),
            pltpu.VMEM((rows, width), jnp.float32),
            pltpu.SemaphoreType.DMA((len(lefts),)),
            pltpu.SemaphoreType.DMA((slots, 4)),
        ],
        compiler_params=pltpu.CompilerParams(vmem_limit_bytes=58 << 20),
        cost_estimate=pl.CostEstimate(
            flops=2 * rows * width * width * count, bytes_accessed=2 * width * count * (rows + width), transcendentals=0
        ),
        name=name,
    )(left_at, right_at, core.astype(jnp.int32)[None], want, *arrays, *extra)


def over_row(value, z_step, y_step, core_step):
    size = lax.axis_size("row")
    pairs = []
    for source in range(size):
        z, y, core = source // 8, source // 2 % 4, source % 2
        target = ((z + z_step) % 2 * 4 + (y + y_step) % 4) * 2 + (core + core_step) % 2
        pairs.append((source, target))
    return lax.ppermute(value, "row", pairs)


def over_col(value, z_step, x_step):
    size = lax.axis_size("col")
    pairs = []
    for source in range(size):
        z, x = source // 4, source % 4
        pairs.append((source, (z + z_step) % 2 * 4 + (x + x_step) % 4))
    return lax.ppermute(value, "col", pairs)


def x_shift(value, step):
    return over_col(value, 0, step)


def y_shift(value, step):
    return over_row(value, 0, step, 0)


def z_swap(value):
    return over_col(value, 1, 0)


def core_swap(value):
    return over_row(value, 0, 0, 1)


def after(values, *earlier):
    return lax.optimization_barrier((values, earlier))[0]


def near(value, shift):
    return shift(value, 1), shift(value, -1)


def far(below, above, shift):
    half = below.shape[0] // 2
    return shift(below[:half], 1), shift(above[half:], -1)


def local(blocks, block_atom, block_col, block_count):
    matrix = local_tile(blocks, block_atom, block_col, block_count)
    rows = matrix.shape[0]
    half = rows // 2
    quarter = half // 2
    row, col = lax.axis_index("row"), lax.axis_index("col")
    z_hi, y, core = row // 8, row // 2 % 4, row % 2
    z_lo, x = col // 4, col % 4

    def col_chunk(z_step, x_step):
        return (z_lo + z_step) % 2 * 4 + (x + x_step) % 4

    def row_chunk(z_step, y_step):
        return (z_hi + z_step) % 2 * 4 + (y + y_step) % 4

    top, bottom = matrix[:half], matrix[half:]
    other_z = over_row(matrix, 1, 0, 0)
    x_near = near(matrix, x_shift)
    y_near = near(matrix, y_shift)
    top, bottom, matrix_b, other_z, x_near, y_near = after((top, bottom, matrix, other_z, x_near, y_near))
    top_z = z_swap(top)
    x_far = far(*x_near, x_shift)
    y_far = far(*y_near, y_shift)
    z_near = near(other_z, y_shift)
    swapped = {}
    swapped["own"] = core_swap(matrix_b)
    swapped["near"] = [core_swap(v) for v in y_near]
    bottom, top_z, x_far = after((bottom, top_z, x_far))
    bottom_z = z_swap(bottom)
    top_z_near = near(top_z, x_shift)
    bottom_z, top_z_near = after((bottom_z, top_z_near))
    top_z_far = far(*top_z_near, x_shift)
    bottom_z_near = near(bottom_z, x_shift)
    z_near, y_far, top_z_far, other_z_b = after((z_near, y_far, top_z_far, other_z))
    z_far = far(*z_near, y_shift)
    swapped["far"] = [core_swap(v) for v in y_far]
    swapped["z"] = core_swap(other_z_b)
    swapped["z near"] = [core_swap(v) for v in z_near]
    bottom_z_near, z_far_b = after((bottom_z_near, z_far))
    bottom_z_far = far(*bottom_z_near, x_shift)
    z_far = z_far_b
    swapped["z far"] = [core_swap(v) for v in z_far]

    pieces = [
        (0, 0, [(matrix, 0)], [(swapped["own"], 0)]),
        (0, -1, [(y_near[0], 0)], [(swapped["near"][0], 0)]),
        (0, 1, [(y_near[1], 0)], [(swapped["near"][1], 0)]),
        (0, 2, [(y_far[0], 0), (y_far[1], half)], [(swapped["far"][0], 0), (swapped["far"][1], half)]),
        (1, 0, [(other_z, 0)], [(swapped["z"], 0)]),
        (1, -1, [(z_near[0], 0)], [(swapped["z near"][0], 0)]),
        (1, 1, [(z_near[1], 0)], [(swapped["z near"][1], 0)]),
        (1, 2, [(z_far[0], 0), (z_far[1], half)], [(swapped["z far"][0], 0), (swapped["z far"][1], half)]),
    ]
    chunks = [(row_chunk(z_step, y_step), mine, others) for z_step, y_step, mine, others in pieces]

    def strip(z_step, own, near_two, far_two, source=0):
        return [
            (own, col_chunk(z_step, 0), source, 0, half),
            (near_two[0], col_chunk(z_step, -1), source, 0, half),
            (near_two[1], col_chunk(z_step, 1), source, 0, half),
            (far_two[0], col_chunk(z_step, 2), 0, 0, quarter),
            (far_two[1], col_chunk(z_step, 2), 0, quarter, quarter),
        ]

    factor = 0.5 / (matrix.shape[1] * lax.axis_size("col"))
    kind = matrix.dtype
    def both(z_step, first, second):
        parts = []
        for below, (own, near_two, far_two) in ((0, first), (half, second)):
            for array, chunk, source, row_at, count in strip(z_step, own, near_two, far_two):
                parts.append((array, chunk, source, row_at + below, count))
        return parts

    lefts = [(value, col_chunk(0, step), 0, 0, rows) for value, step in ((matrix, 0), (x_near[0], -1), (x_near[1], 1))]
    lefts += [(value, col_chunk(0, 2), 0, index * half, half) for index, value in enumerate(x_far)]
    lefts += both(1, (top_z, top_z_near, top_z_far), (bottom_z, bottom_z_near, bottom_z_far))
    h1, h2 = product(lefts, chunks, core, [half, half], factor, kind, "square")
    h2_z, h1_z = z_swap(h2), z_swap(h1)
    h1_near, h2_near = near(h1, x_shift), near(h2, x_shift)
    h1_near, h2_near, h1_z, h2_z, h1, h2 = after((h1_near, h2_near, h1_z, h2_z, h1, h2))
    h1_far = far(*h1_near, x_shift)
    h1_z_near = [z_swap(v) for v in h1_near]
    h1_far, h2_z, h2_near = after((h1_far, h2_z, h2_near))
    h1_z_far = [z_swap(v) for v in h1_far]
    h2_z_near = near(h2_z, x_shift)
    h2_far = far(*h2_near, x_shift)
    h2_z_near, h2_far, h1_z_near = after((h2_z_near, h2_far, h1_z_near))
    h2_z_far = far(*h2_z_near, x_shift)

    lefts = both(0, (h1, h1_near, h1_far), (h2, h2_near, h2_far))
    (total,) = product(lefts, chunks, core, [rows], 1.0, jnp.float32, "step_first", z_lo)
    late = (h1_z, h1_z_near, h1_z_far, h2_z, h2_z_near, h2_z_far)
    h1_z, h1_z_near, h1_z_far, h2_z, h2_z_near, h2_z_far = after(late, total)
    lefts = both(1, (h1_z, h1_z_near, h1_z_far), (h2_z, h2_z_near, h2_z_far))
    (out,) = product(lefts, chunks, core, [rows], 1.0, jnp.float32, "step_last", 1 - z_lo, total, matrix)
    return out


def solution(mesh):
    placed = (P("row", "col", None), P("row", "col"), P("row", "col"), P("row", "col"))
    return jax.shard_map(
        local, mesh=mesh, in_specs=placed, out_specs=P("row", "col"), check_vma=False
    )
```

```python
import functools

import jax
import jax.numpy as jnp
from jax import lax
from jax.experimental import pallas as pl
from jax.experimental.pallas import tpu as pltpu
from jax.sharding import PartitionSpec as P

BLOCK = 128
BR = 4
BC = 8
CAP = 2
META = 16
NONE = 64


def pack_kernel(atom, column, count, blocks, send, seen, place):
    groups = send.shape[0]
    slots = blocks.shape[0]
    send[...] = jnp.zeros_like(send)
    for group in range(groups):
        seen[group] = 0
        for turn in range(CAP):
            place[group * CAP + turn] = NONE

    @pl.loop(0, slots)
    def _(slot):
        @pl.when(slot < count[0, 0])
        def _():
            group = atom[slot] // BR
            turn = jnp.minimum(seen[group], CAP - 1)
            seen[group] = turn + 1
            place[group * CAP + turn] = atom[slot] % BR * BC + column[slot]
            start = pl.multiple_of(turn * BLOCK, BLOCK)
            send[group, pl.ds(start, BLOCK), :] = blocks[slot]

    row = lax.broadcasted_iota(jnp.int32, (META, BLOCK), 0)
    for group in range(groups):
        value = jnp.where(row == 0, place[group * CAP], place[group * CAP + 1])
        send[group, CAP * BLOCK :, :] = value.astype(jnp.float32).astype(send.dtype)


def unpack_kernel(received, tile, place_vector, place, sem):
    owners = received.shape[0]
    tile[...] = jnp.zeros_like(tile)
    lane = lax.broadcasted_iota(jnp.int32, (META, BLOCK), 1)
    places = jnp.full((META, BLOCK), NONE, jnp.int32)
    for owner in range(owners):
        value = received[owner, CAP * BLOCK :, :].astype(jnp.float32).astype(jnp.int32)
        places = jnp.where(lane == owner, value, places)
    place_vector[...] = places
    copy = pltpu.make_async_copy(place_vector, place, sem)
    copy.start()
    copy.wait()

    @pl.loop(0, owners)
    def _(owner):
        for turn in range(CAP):
            at = place[turn, owner]

            @pl.when(at < BR * BC)
            def _():
                top = pl.multiple_of(at // BC * BLOCK, BLOCK)
                left = pl.multiple_of(at % BC * BLOCK, BLOCK)
                block = received[owner, turn * BLOCK : (turn + 1) * BLOCK, :]
                tile[pl.ds(top, BLOCK), pl.ds(left, BLOCK)] = block


def local_tile(blocks, block_atom, block_col, block_count):
    owners = lax.axis_size("row")
    vmem = pl.BlockSpec(memory_space=pltpu.VMEM)
    smem = pl.BlockSpec(memory_space=pltpu.SMEM)
    send = pl.pallas_call(
        pack_kernel,
        out_shape=jax.ShapeDtypeStruct((owners, CAP * BLOCK + META, BLOCK), blocks.dtype),
        in_specs=[smem, smem, smem, vmem],
        out_specs=vmem,
        scratch_shapes=[pltpu.SMEM((owners,), jnp.int32), pltpu.SMEM((owners * CAP,), jnp.int32)],
        compiler_params=pltpu.CompilerParams(vmem_limit_bytes=16 << 20),
        name="pack",
    )(block_atom[:, 0], block_col[:, 0], block_count, blocks)
    received = lax.all_to_all(send, "row", 0, 0, tiled=True)
    return pl.pallas_call(
        unpack_kernel,
        out_shape=jax.ShapeDtypeStruct((BR * BLOCK, BC * BLOCK), blocks.dtype),
        in_specs=[vmem],
        out_specs=vmem,
        scratch_shapes=[
            pltpu.VMEM((META, BLOCK), jnp.int32),
            pltpu.SMEM((META, BLOCK), jnp.int32),
            pltpu.SemaphoreType.DMA,
        ],
        compiler_params=pltpu.CompilerParams(vmem_limit_bytes=16 << 20),
        name="unpack",
    )(received)


def product_kernel(factor, left_parts, right_parts, part, first_total, has_base, n_out, left_at, right_at, core, want, *refs):
    lefts, refs = refs[: len(left_parts)], refs[len(left_parts) :]
    n_right = sum(len(pieces) for chunk in right_parts for pieces in chunk)
    rights, refs = list(refs[:n_right]), refs[n_right:]
    if first_total:
        total_in, refs = refs[0], refs[1:]
    if has_base:
        base, refs = refs[0], refs[1:]
    outs, (held, staged, total, base_held, left_sems, right_sems, extra_sems) = refs[:n_out], refs[n_out:]
    places, (slots, depth, _) = held.shape[0], staged.shape
    copies = []
    for index, (left, (source, first, count)) in enumerate(zip(lefts, left_parts)):
        place = left_at[index] % places
        target = held.at[place, pl.ds(first, count)]
        copies.append(pltpu.make_async_copy(left.at[pl.ds(source, count)], target, left_sems.at[place]))
    loads = []
    for index, chunk in enumerate(right_parts):
        load = []
        for step, pieces in enumerate(chunk):
            down = (core[0] + step) % 2 * (depth // 2)
            for first, count in pieces:
                target = staged.at[index % slots, pl.ds(pl.multiple_of(down + first, count), count)]
                sem = right_sems.at[index % slots]
                load.append(pltpu.make_async_copy(rights.pop(0), target, sem))
        loads.append(load)

    def when_wanted(index, act):
        if part:
            pl.when(right_at[index] // places == want[0])(act)
        else:
            act()

    def start(index):
        for load in loads[index]:
            load.start()
        for at, copy in enumerate(copies):
            pl.when(left_at[at] == right_at[index])(copy.start)

    for index in range(slots - 1):
        when_wanted(index, functools.partial(start, index))
    if first_total:
        total_copy = pltpu.make_async_copy(total_in, total, extra_sems.at[0])
        total_copy.start()
    else:
        total[...] = jnp.zeros_like(total)
    if has_base:
        base_copy = pltpu.make_async_copy(base, base_held, extra_sems.at[1])
        base_copy.start()
    if first_total:
        total_copy.wait()

    @pl.loop(0, len(loads))
    def _(index):
        for ahead in range(slots - 1, len(loads)):

            @pl.when(index == ahead - slots + 1)
            def _():
                when_wanted(ahead, functools.partial(start, ahead))

        def add():
            place, slot = right_at[index] % places, index % slots
            pltpu.make_async_copy(held.at[place], held.at[place], left_sems.at[place]).wait()
            pltpu.make_async_copy(staged.at[slot], staged.at[slot], right_sems.at[slot]).wait()
            total[...] += jnp.dot(held[place], staged[slot], preferred_element_type=jnp.float32)

        when_wanted(index, add)

    if has_base:
        base_copy.wait()
    first = 0
    for out in outs:
        count = out.shape[0]
        value = total[first : first + count, :] * factor
        if has_base:
            value = 1.5 * base_held[first : first + count, :].astype(jnp.float32) - value
        out[...] = value.astype(out.dtype)
        first += count


def product(lefts, rights, core, outs, factor, dtype, name, part=None, first_total=None, base=None):
    width = lefts[0][0].shape[1]
    kind = lefts[0][0].dtype
    left_parts = [(source, first, count) for _, _, source, first, count in lefts]
    right_parts = [
        [[(first, array.shape[0]) for array, first in pieces] for pieces in chunk[1:]] for chunk in rights
    ]
    left_at = jnp.stack([chunk for _, chunk, *_ in lefts]).astype(jnp.int32)
    right_at = jnp.stack([chunk for chunk, *_ in rights]).astype(jnp.int32)
    want = jnp.asarray(0 if part is None else part, jnp.int32)[None]
    smem = pl.BlockSpec(memory_space=pltpu.SMEM)
    vmem = pl.BlockSpec(memory_space=pltpu.VMEM)
    hbm = pl.BlockSpec(memory_space=pltpu.HBM)
    arrays = [left for left, *_ in lefts]
    arrays += [array for chunk in rights for pieces in chunk[1:] for array, _ in pieces]
    extra = [value for value in (first_total, base) if value is not None]
    count = len(rights) if part is None else len(rights) // 2
    rows = sum(outs)
    slots = 5 if part is None else 8
    return pl.pallas_call(
        functools.partial(
            product_kernel,
            factor,
            left_parts,
            right_parts,
            part is not None,
            first_total is not None,
            base is not None,
            len(outs),
        ),
        out_shape=[jax.ShapeDtypeStruct((out, width), dtype) for out in outs],
        in_specs=[smem] * 4 + [hbm] * (len(arrays) + len(extra)),
        out_specs=[vmem] * len(outs),
        scratch_shapes=[
            pltpu.VMEM((count, rows, width), kind),
            pltpu.VMEM((slots, width, width), kind),
            pltpu.VMEM((rows, width), jnp.float32),
            pltpu.VMEM((rows, width), kind),
            pltpu.SemaphoreType.DMA((count,)),
            pltpu.SemaphoreType.DMA((slots,)),
            pltpu.SemaphoreType.DMA((2,)),
        ],
        compiler_params=pltpu.CompilerParams(vmem_limit_bytes=58 << 20),
        cost_estimate=pl.CostEstimate(
            flops=2 * rows * width * width * count, bytes_accessed=2 * width * count * (rows + width), transcendentals=0
        ),
        name=name,
    )(left_at, right_at, core.astype(jnp.int32)[None], want, *arrays, *extra)


def over_row(value, z_step, y_step, core_step):
    size = lax.axis_size("row")
    pairs = []
    for source in range(size):
        z, y, core = source // 8, source // 2 % 4, source % 2
        target = ((z + z_step) % 2 * 4 + (y + y_step) % 4) * 2 + (core + core_step) % 2
        pairs.append((source, target))
    return lax.ppermute(value, "row", pairs)


def over_col(value, z_step, x_step):
    size = lax.axis_size("col")
    pairs = []
    for source in range(size):
        z, x = source // 4, source % 4
        pairs.append((source, (z + z_step) % 2 * 4 + (x + x_step) % 4))
    return lax.ppermute(value, "col", pairs)


def x_shift(value, step):
    return over_col(value, 0, step)


def y_shift(value, step):
    return over_row(value, 0, step, 0)


def z_swap(value):
    return over_col(value, 1, 0)


def core_swap(value):
    return over_row(value, 0, 0, 1)


def after(values, *earlier):
    return lax.optimization_barrier((values, earlier))[0]


def near(value, shift):
    return shift(value, 1), shift(value, -1)


def far(below, above, shift):
    half = below.shape[0] // 2
    return shift(below[:half], 1), shift(above[half:], -1)


def local(blocks, block_atom, block_col, block_count):
    matrix = local_tile(blocks, block_atom, block_col, block_count)
    rows = matrix.shape[0]
    half = rows // 2
    quarter = half // 2
    row, col = lax.axis_index("row"), lax.axis_index("col")
    z_hi, y, core = row // 8, row // 2 % 4, row % 2
    z_lo, x = col // 4, col % 4

    def col_chunk(z_step, x_step):
        return (z_lo + z_step) % 2 * 4 + (x + x_step) % 4

    def row_chunk(z_step, y_step):
        return (z_hi + z_step) % 2 * 4 + (y + y_step) % 4

    top, bottom = matrix[:half], matrix[half:]
    other_z = over_row(matrix, 1, 0, 0)
    x_near = near(matrix, x_shift)
    y_near = near(matrix, y_shift)
    top, bottom, matrix_b, other_z, x_near, y_near = after((top, bottom, matrix, other_z, x_near, y_near))
    top_z = z_swap(top)
    x_far = far(*x_near, x_shift)
    y_far = far(*y_near, y_shift)
    swapped = {}
    swapped["own"] = core_swap(matrix_b)
    swapped["near"] = [core_swap(v) for v in y_near]
    bottom, top_z, x_far, y_far, other_z = after((bottom, top_z, x_far, y_far, other_z))
    w1, w2 = other_z[:half], other_z[half:]
    wm1, wp2 = y_shift(w1, 1), y_shift(w2, -1)
    bottom_z = z_swap(bottom)
    top_z_near = near(top_z, x_shift)
    bottom_z, top_z_near, wm1, wp2, w1, w2 = after((bottom_z, top_z_near, wm1, wp2, w1, w2))
    wm2, wp1 = y_shift(w2, 1), y_shift(w1, -1)
    bottom_z_near = near(bottom_z, x_shift)
    cross_top = x_shift(top_z_near[0], 1)
    wm1, wp2, wm2, wp1, bottom_z_near, y_far, other_z = after(
        (wm1, wp2, wm2, wp1, bottom_z_near, y_far, other_z)
    )
    z_far = y_shift(wm1, 1), y_shift(wp2, -1)
    cross_bottom = x_shift(bottom_z_near[1], -1)
    swapped["z"] = core_swap(other_z)
    swapped["far"] = [core_swap(v) for v in y_far]
    z_near = [(wm1, wm2), (wp1, wp2)]
    swapped["z near"] = [[core_swap(v) for v in pair] for pair in z_near]
    z_far, cross_bottom = after((z_far, cross_bottom))
    z_cross = cross_top, cross_bottom
    swapped["z far"] = [core_swap(v) for v in z_far]

    def in_two(pair):
        return [(pair[0], 0), (pair[1], half)]

    pieces = [
        (0, 0, [(matrix, 0)], [(swapped["own"], 0)]),
        (0, -1, [(y_near[0], 0)], [(swapped["near"][0], 0)]),
        (0, 1, [(y_near[1], 0)], [(swapped["near"][1], 0)]),
        (0, 2, [(y_far[0], 0), (y_far[1], half)], [(swapped["far"][0], 0), (swapped["far"][1], half)]),
        (1, 0, [(other_z, 0)], [(swapped["z"], 0)]),
        (1, -1, in_two(z_near[0]), in_two(swapped["z near"][0])),
        (1, 1, in_two(z_near[1]), in_two(swapped["z near"][1])),
        (1, 2, [(z_far[0], 0), (z_far[1], half)], [(swapped["z far"][0], 0), (swapped["z far"][1], half)]),
    ]
    chunks = [(row_chunk(z_step, y_step), mine, others) for z_step, y_step, mine, others in pieces]

    def strip(z_step, own, near_two, far_parts):
        parts = [
            (value, col_chunk(z_step, step), 0, 0, half) for value, step in zip((own, *near_two), (0, -1, 1))
        ]
        count = half // len(far_parts)
        return parts + [
            (value, col_chunk(z_step, 2), 0, index * count, count) for index, value in enumerate(far_parts)
        ]

    factor = 0.5 / (matrix.shape[1] * lax.axis_size("col"))
    kind = matrix.dtype
    def both(z_step, first, second):
        parts = []
        for below, (own, near_two, far_two) in ((0, first), (half, second)):
            for array, chunk, source, row_at, count in strip(z_step, own, near_two, far_two):
                parts.append((array, chunk, source, row_at + below, count))
        return parts

    lefts = [(value, col_chunk(0, step), 0, 0, rows) for value, step in ((matrix, 0), (x_near[0], -1), (x_near[1], 1))]
    lefts += [(value, col_chunk(0, 2), 0, index * half, half) for index, value in enumerate(x_far)]
    for below, own, two, cross in ((0, top_z, top_z_near, z_cross[0]), (half, bottom_z, bottom_z_near, z_cross[1])):
        for value, step in ((own, 0), (two[0], -1), (two[1], 1), (cross, 2)):
            lefts.append((value, col_chunk(1, step), 0, below, half))
    h1, h2 = product(lefts, chunks, core, [half, half], factor, kind, "square")
    h2_z, h1_z = z_swap(h2), z_swap(h1)
    h1_near, h2_near = near(h1, x_shift), near(h2, x_shift)
    h1_near, h2_near, h1_z, h2_z, h1, h2 = after((h1_near, h2_near, h1_z, h2_z, h1, h2))
    h1_far, h2_far = x_shift(h1_near[0], 1), x_shift(h2_near[1], -1)
    h1_z_near = [z_swap(v) for v in h1_near]
    h1_far, h2_far, h2_z = after((h1_far, h2_far, h2_z))
    h2_z_near = near(h2_z, x_shift)
    h1_z_far = z_swap(h1_far)
    h2_z_near, h1_z_near = after((h2_z_near, h1_z_near))
    h2_z_far = far(*h2_z_near, x_shift)
    h1_far, h2_far, h1_z_far = [h1_far], [h2_far], [h1_z_far]

    lefts = both(0, (h1, h1_near, h1_far), (h2, h2_near, h2_far))
    (total,) = product(lefts, chunks, core, [rows], 1.0, jnp.float32, "step_first", z_lo)
    late = (h1_z, h1_z_near, h1_z_far, h2_z, h2_z_near, h2_z_far)
    h1_z, h1_z_near, h1_z_far, h2_z, h2_z_near, h2_z_far = after(late, total)
    lefts = both(1, (h1_z, h1_z_near, h1_z_far), (h2_z, h2_z_near, h2_z_far))
    (out,) = product(lefts, chunks, core, [rows], 1.0, jnp.float32, "step_last", 1 - z_lo, total, matrix)
    return out


def solution(mesh):
    placed = (P("row", "col", None), P("row", "col"), P("row", "col"), P("row", "col"))
    return jax.shard_map(
        local, mesh=mesh, in_specs=placed, out_specs=P("row", "col"), check_vma=False
    )
```

```python
import functools

import jax
import jax.numpy as jnp
from jax import lax
from jax.experimental import pallas as pl
from jax.experimental.pallas import tpu as pltpu
from jax.sharding import PartitionSpec as P

BLOCK = 128
BR = 4
BC = 8
CAP = 2
META = 16
NONE = 64


def pack_kernel(atom, column, count, blocks, send, seen, place):
    groups = send.shape[0]
    slots = blocks.shape[0]
    send[...] = jnp.zeros_like(send)
    for group in range(groups):
        seen[group] = 0
        for turn in range(CAP):
            place[group * CAP + turn] = NONE

    @pl.loop(0, slots)
    def _(slot):
        @pl.when(slot < count[0, 0])
        def _():
            group = atom[slot] // BR
            turn = jnp.minimum(seen[group], CAP - 1)
            seen[group] = turn + 1
            place[group * CAP + turn] = atom[slot] % BR * BC + column[slot]
            start = pl.multiple_of(turn * BLOCK, BLOCK)
            send[group, pl.ds(start, BLOCK), :] = blocks[slot]

    row = lax.broadcasted_iota(jnp.int32, (META, BLOCK), 0)
    for group in range(groups):
        value = jnp.where(row == 0, place[group * CAP], place[group * CAP + 1])
        send[group, CAP * BLOCK :, :] = value.astype(jnp.float32).astype(send.dtype)


def unpack_kernel(received, tile, place_vector, place, sem):
    owners = received.shape[0]
    tile[...] = jnp.zeros_like(tile)
    lane = lax.broadcasted_iota(jnp.int32, (META, BLOCK), 1)
    places = jnp.full((META, BLOCK), NONE, jnp.int32)
    for owner in range(owners):
        value = received[owner, CAP * BLOCK :, :].astype(jnp.float32).astype(jnp.int32)
        places = jnp.where(lane == owner, value, places)
    place_vector[...] = places
    copy = pltpu.make_async_copy(place_vector, place, sem)
    copy.start()
    copy.wait()

    @pl.loop(0, owners)
    def _(owner):
        for turn in range(CAP):
            at = place[turn, owner]

            @pl.when(at < BR * BC)
            def _():
                top = pl.multiple_of(at // BC * BLOCK, BLOCK)
                left = pl.multiple_of(at % BC * BLOCK, BLOCK)
                block = received[owner, turn * BLOCK : (turn + 1) * BLOCK, :]
                tile[pl.ds(top, BLOCK), pl.ds(left, BLOCK)] = block


def local_tile(blocks, block_atom, block_col, block_count):
    owners = lax.axis_size("row")
    vmem = pl.BlockSpec(memory_space=pltpu.VMEM)
    smem = pl.BlockSpec(memory_space=pltpu.SMEM)
    send = pl.pallas_call(
        pack_kernel,
        out_shape=jax.ShapeDtypeStruct((owners, CAP * BLOCK + META, BLOCK), blocks.dtype),
        in_specs=[smem, smem, smem, vmem],
        out_specs=vmem,
        scratch_shapes=[pltpu.SMEM((owners,), jnp.int32), pltpu.SMEM((owners * CAP,), jnp.int32)],
        compiler_params=pltpu.CompilerParams(vmem_limit_bytes=16 << 20),
        name="pack",
    )(block_atom[:, 0], block_col[:, 0], block_count, blocks)
    received = lax.all_to_all(send, "row", 0, 0, tiled=True)
    return pl.pallas_call(
        unpack_kernel,
        out_shape=jax.ShapeDtypeStruct((BR * BLOCK, BC * BLOCK), blocks.dtype),
        in_specs=[vmem],
        out_specs=vmem,
        scratch_shapes=[
            pltpu.VMEM((META, BLOCK), jnp.int32),
            pltpu.SMEM((META, BLOCK), jnp.int32),
            pltpu.SemaphoreType.DMA,
        ],
        compiler_params=pltpu.CompilerParams(vmem_limit_bytes=16 << 20),
        name="unpack",
    )(received)


def product_kernel(factor, left_parts, right_parts, part, first_total, has_base, n_out, left_at, right_at, core, want, *refs):
    lefts, refs = refs[: len(left_parts)], refs[len(left_parts) :]
    n_right = sum(len(pieces) for chunk in right_parts for pieces in chunk)
    rights, refs = list(refs[:n_right]), refs[n_right:]
    if first_total:
        total_in, refs = refs[0], refs[1:]
    if has_base:
        base, refs = refs[0], refs[1:]
    outs, (held, staged, total, base_held, left_sems, right_sems, extra_sems) = refs[:n_out], refs[n_out:]
    places, (slots, depth, _) = held.shape[0], staged.shape
    copies = []
    for index, (left, (source, first, count)) in enumerate(zip(lefts, left_parts)):
        place = left_at[index] % places
        target = held.at[place, pl.ds(first, count)]
        copies.append(pltpu.make_async_copy(left.at[pl.ds(source, count)], target, left_sems.at[place]))
    loads = []
    for index, chunk in enumerate(right_parts):
        load = []
        for step, pieces in enumerate(chunk):
            down = (core[0] + step) % 2 * (depth // 2)
            for first, count in pieces:
                target = staged.at[index % slots, pl.ds(pl.multiple_of(down + first, count), count)]
                sem = right_sems.at[index % slots]
                load.append(pltpu.make_async_copy(rights.pop(0), target, sem))
        loads.append(load)

    def when_wanted(index, act):
        if part:
            pl.when(right_at[index] // places == want[0])(act)
        else:
            act()

    def start(index):
        for load in loads[index]:
            load.start()
        for at, copy in enumerate(copies):
            pl.when(left_at[at] == right_at[index])(copy.start)

    for index in range(slots - 1):
        when_wanted(index, functools.partial(start, index))
    if first_total:
        total_copy = pltpu.make_async_copy(total_in, total, extra_sems.at[0])
        total_copy.start()
    else:
        total[...] = jnp.zeros_like(total)
    if has_base:
        base_copy = pltpu.make_async_copy(base, base_held, extra_sems.at[1])
        base_copy.start()
    if first_total:
        total_copy.wait()

    @pl.loop(0, len(loads))
    def _(index):
        for ahead in range(slots - 1, len(loads)):

            @pl.when(index == ahead - slots + 1)
            def _():
                when_wanted(ahead, functools.partial(start, ahead))

        def add():
            place, slot = right_at[index] % places, index % slots
            pltpu.make_async_copy(held.at[place], held.at[place], left_sems.at[place]).wait()
            pltpu.make_async_copy(staged.at[slot], staged.at[slot], right_sems.at[slot]).wait()
            total[...] += jnp.dot(held[place], staged[slot], preferred_element_type=jnp.float32)

        when_wanted(index, add)

    if has_base:
        base_copy.wait()
    first = 0
    for out in outs:
        count = out.shape[0]
        value = total[first : first + count, :] * factor
        if has_base:
            value = 1.5 * base_held[first : first + count, :].astype(jnp.float32) - value
        out[...] = value.astype(out.dtype)
        first += count


def product(lefts, rights, core, outs, factor, dtype, name, part=None, first_total=None, base=None):
    width = lefts[0][0].shape[1]
    kind = lefts[0][0].dtype
    left_parts = [(source, first, count) for _, _, source, first, count in lefts]
    right_parts = [
        [[(first, array.shape[0]) for array, first in pieces] for pieces in chunk[1:]] for chunk in rights
    ]
    left_at = jnp.stack([chunk for _, chunk, *_ in lefts]).astype(jnp.int32)
    right_at = jnp.stack([chunk for chunk, *_ in rights]).astype(jnp.int32)
    want = jnp.asarray(0 if part is None else part, jnp.int32)[None]
    smem = pl.BlockSpec(memory_space=pltpu.SMEM)
    vmem = pl.BlockSpec(memory_space=pltpu.VMEM)
    hbm = pl.BlockSpec(memory_space=pltpu.HBM)
    arrays = [left for left, *_ in lefts]
    arrays += [array for chunk in rights for pieces in chunk[1:] for array, _ in pieces]
    extra = [value for value in (first_total, base) if value is not None]
    count = len(rights) if part is None else len(rights) // 2
    rows = sum(outs)
    slots = 5 if part is None else 8
    return pl.pallas_call(
        functools.partial(
            product_kernel,
            factor,
            left_parts,
            right_parts,
            part is not None,
            first_total is not None,
            base is not None,
            len(outs),
        ),
        out_shape=[jax.ShapeDtypeStruct((out, width), dtype) for out in outs],
        in_specs=[smem] * 4 + [hbm] * (len(arrays) + len(extra)),
        out_specs=[vmem] * len(outs),
        scratch_shapes=[
            pltpu.VMEM((count, rows, width), kind),
            pltpu.VMEM((slots, width, width), kind),
            pltpu.VMEM((rows, width), jnp.float32),
            pltpu.VMEM((rows, width), kind),
            pltpu.SemaphoreType.DMA((count,)),
            pltpu.SemaphoreType.DMA((slots,)),
            pltpu.SemaphoreType.DMA((2,)),
        ],
        compiler_params=pltpu.CompilerParams(vmem_limit_bytes=58 << 20),
        cost_estimate=pl.CostEstimate(
            flops=2 * rows * width * width * count, bytes_accessed=2 * width * count * (rows + width), transcendentals=0
        ),
        name=name,
    )(left_at, right_at, core.astype(jnp.int32)[None], want, *arrays, *extra)


def over_row(value, z_step, y_step, core_step):
    size = lax.axis_size("row")
    pairs = []
    for source in range(size):
        z, y, core = source // 8, source // 2 % 4, source % 2
        target = ((z + z_step) % 2 * 4 + (y + y_step) % 4) * 2 + (core + core_step) % 2
        pairs.append((source, target))
    return lax.ppermute(value, "row", pairs)


def over_col(value, z_step, x_step):
    size = lax.axis_size("col")
    pairs = []
    for source in range(size):
        z, x = source // 4, source % 4
        pairs.append((source, (z + z_step) % 2 * 4 + (x + x_step) % 4))
    return lax.ppermute(value, "col", pairs)


def x_shift(value, step):
    return over_col(value, 0, step)


def y_shift(value, step):
    return over_row(value, 0, step, 0)


def z_swap(value):
    return over_col(value, 1, 0)


def core_swap(value):
    return over_row(value, 0, 0, 1)


def after(values, *earlier):
    return lax.optimization_barrier((values, earlier))[0]


def near(value, shift):
    return shift(value, 1), shift(value, -1)


def far(below, above, shift):
    half = below.shape[0] // 2
    return shift(below[:half], 1), shift(above[half:], -1)


def local(blocks, block_atom, block_col, block_count):
    matrix = local_tile(blocks, block_atom, block_col, block_count)
    rows = matrix.shape[0]
    half = rows // 2
    quarter = half // 2
    row, col = lax.axis_index("row"), lax.axis_index("col")
    z_hi, y, core = row // 8, row // 2 % 4, row % 2
    z_lo, x = col // 4, col % 4

    def col_chunk(z_step, x_step):
        return (z_lo + z_step) % 2 * 4 + (x + x_step) % 4

    def row_chunk(z_step, y_step):
        return (z_hi + z_step) % 2 * 4 + (y + y_step) % 4

    top, bottom = matrix[:half], matrix[half:]
    other_z = over_row(matrix, 1, 0, 0)
    x_near = near(matrix, x_shift)
    y_near = near(matrix, y_shift)
    top, bottom, matrix_b, other_z, x_near, y_near = after((top, bottom, matrix, other_z, x_near, y_near))
    top_z = z_swap(top)
    x_far = far(*x_near, x_shift)
    y_far = far(*y_near, y_shift)
    swapped = {}
    swapped["own"] = core_swap(matrix_b)
    swapped["near"] = [core_swap(v) for v in y_near]
    bottom, top_z, x_far, y_far, other_z = after((bottom, top_z, x_far, y_far, other_z))
    w1, w2 = other_z[:half], other_z[half:]
    wm1, wp2 = y_shift(w1, 1), y_shift(w2, -1)
    bottom_z = z_swap(bottom)
    top_z_near = near(top_z, x_shift)
    bottom_z, top_z_near, wm1, wp2, w1, w2 = after((bottom_z, top_z_near, wm1, wp2, w1, w2))
    wm2, wp1 = y_shift(w2, 1), y_shift(w1, -1)
    bottom_z_near = near(bottom_z, x_shift)
    cross_top = x_shift(top_z_near[0], 1)
    wm1, wp2, wm2, wp1, bottom_z_near, y_far, other_z = after(
        (wm1, wp2, wm2, wp1, bottom_z_near, y_far, other_z)
    )
    z_far = y_shift(wm1, 1), y_shift(wp2, -1)
    cross_bottom = x_shift(bottom_z_near[1], -1)
    swapped["z"] = core_swap(other_z)
    swapped["far"] = [core_swap(v) for v in y_far]
    z_near = [(wm1, wm2), (wp1, wp2)]
    swapped["z near"] = [[core_swap(v) for v in pair] for pair in z_near]
    z_far, cross_bottom = after((z_far, cross_bottom))
    z_cross = cross_top, cross_bottom
    swapped["z far"] = [core_swap(v) for v in z_far]

    def in_two(pair):
        return [(pair[0], 0), (pair[1], half)]

    pieces = [
        (0, 0, [(matrix, 0)], [(swapped["own"], 0)]),
        (0, -1, [(y_near[0], 0)], [(swapped["near"][0], 0)]),
        (0, 1, [(y_near[1], 0)], [(swapped["near"][1], 0)]),
        (0, 2, [(y_far[0], 0), (y_far[1], half)], [(swapped["far"][0], 0), (swapped["far"][1], half)]),
        (1, 0, [(other_z, 0)], [(swapped["z"], 0)]),
        (1, -1, in_two(z_near[0]), in_two(swapped["z near"][0])),
        (1, 1, in_two(z_near[1]), in_two(swapped["z near"][1])),
        (1, 2, [(z_far[0], 0), (z_far[1], half)], [(swapped["z far"][0], 0), (swapped["z far"][1], half)]),
    ]
    chunks = [(row_chunk(z_step, y_step), mine, others) for z_step, y_step, mine, others in pieces]

    def strip(z_step, own, near_two, far_parts):
        parts = [
            (value, col_chunk(z_step, step), 0, 0, half) for value, step in zip((own, *near_two), (0, -1, 1))
        ]
        count = half // len(far_parts)
        return parts + [
            (value, col_chunk(z_step, 2), 0, index * count, count) for index, value in enumerate(far_parts)
        ]

    factor = 0.5 / (matrix.shape[1] * lax.axis_size("col"))
    kind = matrix.dtype
    def both(z_step, first, second):
        parts = []
        for below, (own, near_two, far_two) in ((0, first), (half, second)):
            for array, chunk, source, row_at, count in strip(z_step, own, near_two, far_two):
                parts.append((array, chunk, source, row_at + below, count))
        return parts

    lefts = [(value, col_chunk(0, step), 0, 0, rows) for value, step in ((matrix, 0), (x_near[0], -1), (x_near[1], 1))]
    lefts += [(value, col_chunk(0, 2), 0, index * half, half) for index, value in enumerate(x_far)]
    for below, own, two, cross in ((0, top_z, top_z_near, z_cross[0]), (half, bottom_z, bottom_z_near, z_cross[1])):
        for value, step in ((own, 0), (two[0], -1), (two[1], 1), (cross, 2)):
            lefts.append((value, col_chunk(1, step), 0, below, half))
    h1, h2 = product(lefts, chunks, core, [half, half], factor, kind, "square")
    h2_z, h1_z = z_swap(h2), z_swap(h1)
    h1_near, h2_near = near(h1, x_shift), near(h2, x_shift)
    h1_near, h2_near, h1_z, h2_z, h1, h2 = after((h1_near, h2_near, h1_z, h2_z, h1, h2))
    h1_far, h2_far = x_shift(h1_near[0], 1), x_shift(h2_near[1], -1)
    h1_z_near = [z_swap(v) for v in h1_near]
    h1_far, h2_far, h2_z = after((h1_far, h2_far, h2_z))
    h2_z_near = near(h2_z, x_shift)
    h1_z_far = z_swap(h1_far)
    lefts = both(0, (h1, h1_near, [h1_far]), (h2, h2_near, [h2_far]))
    (total,) = product(lefts, chunks, core, [rows], 1.0, jnp.float32, "step_first", z_lo)
    h2_z_near, h1_z_near, total = after((h2_z_near, h1_z_near, total))
    h2_z_far = far(*h2_z_near, x_shift)
    h1_z_far = [h1_z_far]
    late = (h1_z, h1_z_near, h1_z_far, h2_z, h2_z_near, h2_z_far)
    h1_z, h1_z_near, h1_z_far, h2_z, h2_z_near, h2_z_far = after(late, total)
    lefts = both(1, (h1_z, h1_z_near, h1_z_far), (h2_z, h2_z_near, h2_z_far))
    (out,) = product(lefts, chunks, core, [rows], 1.0, jnp.float32, "step_last", 1 - z_lo, total, matrix)
    return out


def solution(mesh):
    placed = (P("row", "col", None), P("row", "col"), P("row", "col"), P("row", "col"))
    return jax.shard_map(
        local, mesh=mesh, in_specs=placed, out_specs=P("row", "col"), check_vma=False
    )
```

```python
import functools

import jax
import jax.numpy as jnp
from jax import lax
from jax.experimental import pallas as pl
from jax.experimental.pallas import tpu as pltpu
from jax.sharding import PartitionSpec as P

BLOCK = 128
BR = 4
BC = 8
CAP = 2
META = 16
NONE = 64


def pack_kernel(atom, column, count, blocks, send, seen, place):
    groups = send.shape[0]
    slots = blocks.shape[0]
    send[...] = jnp.zeros_like(send)
    for group in range(groups):
        seen[group] = 0
        for turn in range(CAP):
            place[group * CAP + turn] = NONE

    @pl.loop(0, slots)
    def _(slot):
        @pl.when(slot < count[0, 0])
        def _():
            group = atom[slot] // BR
            turn = jnp.minimum(seen[group], CAP - 1)
            seen[group] = turn + 1
            place[group * CAP + turn] = atom[slot] % BR * BC + column[slot]
            start = pl.multiple_of(turn * BLOCK, BLOCK)
            send[group, pl.ds(start, BLOCK), :] = blocks[slot]

    row = lax.broadcasted_iota(jnp.int32, (META, BLOCK), 0)
    for group in range(groups):
        value = jnp.where(row == 0, place[group * CAP], place[group * CAP + 1])
        send[group, CAP * BLOCK :, :] = value.astype(jnp.float32).astype(send.dtype)


def unpack_kernel(received, tile, place_vector, place, sem):
    owners = received.shape[0]
    tile[...] = jnp.zeros_like(tile)
    lane = lax.broadcasted_iota(jnp.int32, (META, BLOCK), 1)
    places = jnp.full((META, BLOCK), NONE, jnp.int32)
    for owner in range(owners):
        value = received[owner, CAP * BLOCK :, :].astype(jnp.float32).astype(jnp.int32)
        places = jnp.where(lane == owner, value, places)
    place_vector[...] = places
    copy = pltpu.make_async_copy(place_vector, place, sem)
    copy.start()
    copy.wait()

    @pl.loop(0, owners)
    def _(owner):
        for turn in range(CAP):
            at = place[turn, owner]

            @pl.when(at < BR * BC)
            def _():
                top = pl.multiple_of(at // BC * BLOCK, BLOCK)
                left = pl.multiple_of(at % BC * BLOCK, BLOCK)
                block = received[owner, turn * BLOCK : (turn + 1) * BLOCK, :]
                tile[pl.ds(top, BLOCK), pl.ds(left, BLOCK)] = block


def local_tile(blocks, block_atom, block_col, block_count):
    owners = lax.axis_size("row")
    vmem = pl.BlockSpec(memory_space=pltpu.VMEM)
    smem = pl.BlockSpec(memory_space=pltpu.SMEM)
    send = pl.pallas_call(
        pack_kernel,
        out_shape=jax.ShapeDtypeStruct((owners, CAP * BLOCK + META, BLOCK), blocks.dtype),
        in_specs=[smem, smem, smem, vmem],
        out_specs=vmem,
        scratch_shapes=[pltpu.SMEM((owners,), jnp.int32), pltpu.SMEM((owners * CAP,), jnp.int32)],
        compiler_params=pltpu.CompilerParams(vmem_limit_bytes=16 << 20),
        name="pack",
    )(block_atom[:, 0], block_col[:, 0], block_count, blocks)
    received = lax.all_to_all(send, "row", 0, 0, tiled=True)
    return pl.pallas_call(
        unpack_kernel,
        out_shape=jax.ShapeDtypeStruct((BR * BLOCK, BC * BLOCK), blocks.dtype),
        in_specs=[vmem],
        out_specs=vmem,
        scratch_shapes=[
            pltpu.VMEM((META, BLOCK), jnp.int32),
            pltpu.SMEM((META, BLOCK), jnp.int32),
            pltpu.SemaphoreType.DMA,
        ],
        compiler_params=pltpu.CompilerParams(vmem_limit_bytes=16 << 20),
        name="unpack",
    )(received)


def product_kernel(factor, left_parts, right_parts, part, first_total, has_base, n_out, left_at, right_at, core, want, *refs):
    lefts, refs = refs[: len(left_parts)], refs[len(left_parts) :]
    n_right = sum(len(pieces) for chunk in right_parts for pieces in chunk)
    rights, refs = list(refs[:n_right]), refs[n_right:]
    if first_total:
        total_in, refs = refs[0], refs[1:]
    if has_base:
        base, refs = refs[0], refs[1:]
    outs, (held, staged, total, total_held, base_held, left_sems, right_sems, extra_sems) = refs[:n_out], refs[n_out:]
    places, (slots, depth, _) = held.shape[0], staged.shape
    copies = []
    for index, (left, (source, first, count)) in enumerate(zip(lefts, left_parts)):
        place = left_at[index] % places
        target = held.at[place, pl.ds(first, count)]
        copies.append(pltpu.make_async_copy(left.at[pl.ds(source, count)], target, left_sems.at[place]))
    loads = []
    for index, chunk in enumerate(right_parts):
        load = []
        for step, pieces in enumerate(chunk):
            down = (core[0] + step) % 2 * (depth // 2)
            for first, count in pieces:
                target = staged.at[index % slots, pl.ds(pl.multiple_of(down + first, count), count)]
                sem = right_sems.at[index % slots]
                load.append(pltpu.make_async_copy(rights.pop(0), target, sem))
        loads.append(load)

    def when_wanted(index, act):
        if part:
            pl.when(right_at[index] // places == want[0])(act)
        else:
            act()

    def start(index):
        for load in loads[index]:
            load.start()
        for at, copy in enumerate(copies):
            pl.when(left_at[at] == right_at[index])(copy.start)

    for index in range(slots - 1):
        when_wanted(index, functools.partial(start, index))
    total[...] = jnp.zeros_like(total)
    if first_total:
        total_copy = pltpu.make_async_copy(total_in, total_held, extra_sems.at[0])
        total_copy.start()
    if has_base:
        base_copy = pltpu.make_async_copy(base, base_held, extra_sems.at[1])
        base_copy.start()

    @pl.loop(0, len(loads))
    def _(index):
        for ahead in range(slots - 1, len(loads)):

            @pl.when(index == ahead - slots + 1)
            def _():
                when_wanted(ahead, functools.partial(start, ahead))

        def add():
            place, slot = right_at[index] % places, index % slots
            pltpu.make_async_copy(held.at[place], held.at[place], left_sems.at[place]).wait()
            pltpu.make_async_copy(staged.at[slot], staged.at[slot], right_sems.at[slot]).wait()
            total[...] += jnp.dot(held[place], staged[slot], preferred_element_type=jnp.float32)

        when_wanted(index, add)

    if first_total:
        total_copy.wait()
    if has_base:
        base_copy.wait()
    first = 0
    for out in outs:
        count = out.shape[0]
        value = total[first : first + count, :]
        if first_total:
            value += total_held[first : first + count, :]
        value *= factor
        if has_base:
            value = 1.5 * base_held[first : first + count, :].astype(jnp.float32) - value
        out[...] = value.astype(out.dtype)
        first += count


def product(lefts, rights, core, outs, factor, dtype, name, part=None, first_total=None, base=None):
    width = lefts[0][0].shape[1]
    kind = lefts[0][0].dtype
    left_parts = [(source, first, count) for _, _, source, first, count in lefts]
    right_parts = [
        [[(first, array.shape[0]) for array, first in pieces] for pieces in chunk[1:]] for chunk in rights
    ]
    left_at = jnp.stack([chunk for _, chunk, *_ in lefts]).astype(jnp.int32)
    right_at = jnp.stack([chunk for chunk, *_ in rights]).astype(jnp.int32)
    want = jnp.asarray(0 if part is None else part, jnp.int32)[None]
    smem = pl.BlockSpec(memory_space=pltpu.SMEM)
    vmem = pl.BlockSpec(memory_space=pltpu.VMEM)
    hbm = pl.BlockSpec(memory_space=pltpu.HBM)
    arrays = [left for left, *_ in lefts]
    arrays += [array for chunk in rights for pieces in chunk[1:] for array, _ in pieces]
    extra = [value for value in (first_total, base) if value is not None]
    count = len(rights) if part is None else len(rights) // 2
    rows = sum(outs)
    slots = 3
    return pl.pallas_call(
        functools.partial(
            product_kernel,
            factor,
            left_parts,
            right_parts,
            part is not None,
            first_total is not None,
            base is not None,
            len(outs),
        ),
        out_shape=[jax.ShapeDtypeStruct((out, width), dtype) for out in outs],
        in_specs=[smem] * 4 + [hbm] * (len(arrays) + len(extra)),
        out_specs=[vmem] * len(outs),
        scratch_shapes=[
            pltpu.VMEM((count, rows, width), kind),
            pltpu.VMEM((slots, width, width), kind),
            pltpu.VMEM((rows, width), jnp.float32),
            pltpu.VMEM((rows, width), jnp.float32),
            pltpu.VMEM((rows, width), kind),
            pltpu.SemaphoreType.DMA((count,)),
            pltpu.SemaphoreType.DMA((slots,)),
            pltpu.SemaphoreType.DMA((2,)),
        ],
        compiler_params=pltpu.CompilerParams(vmem_limit_bytes=58 << 20),
        cost_estimate=pl.CostEstimate(
            flops=2 * rows * width * width * count, bytes_accessed=2 * width * count * (rows + width), transcendentals=0
        ),
        name=name,
    )(left_at, right_at, core.astype(jnp.int32)[None], want, *arrays, *extra)


def over_row(value, z_step, y_step, core_step):
    size = lax.axis_size("row")
    pairs = []
    for source in range(size):
        z, y, core = source // 8, source // 2 % 4, source % 2
        target = ((z + z_step) % 2 * 4 + (y + y_step) % 4) * 2 + (core + core_step) % 2
        pairs.append((source, target))
    return lax.ppermute(value, "row", pairs)


def over_col(value, z_step, x_step):
    size = lax.axis_size("col")
    pairs = []
    for source in range(size):
        z, x = source // 4, source % 4
        pairs.append((source, (z + z_step) % 2 * 4 + (x + x_step) % 4))
    return lax.ppermute(value, "col", pairs)


def x_shift(value, step):
    return over_col(value, 0, step)


def y_shift(value, step):
    return over_row(value, 0, step, 0)


def z_swap(value):
    return over_col(value, 1, 0)


def core_swap(value):
    return over_row(value, 0, 0, 1)


def after(values, *earlier):
    return lax.optimization_barrier((values, earlier))[0]


def near(value, shift):
    return shift(value, 1), shift(value, -1)


def far(below, above, shift):
    half = below.shape[0] // 2
    return shift(below[:half], 1), shift(above[half:], -1)


def local(blocks, block_atom, block_col, block_count):
    matrix = local_tile(blocks, block_atom, block_col, block_count)
    rows = matrix.shape[0]
    half = rows // 2
    quarter = half // 2
    row, col = lax.axis_index("row"), lax.axis_index("col")
    z_hi, y, core = row // 8, row // 2 % 4, row % 2
    z_lo, x = col // 4, col % 4

    def col_chunk(z_step, x_step):
        return (z_lo + z_step) % 2 * 4 + (x + x_step) % 4

    def row_chunk(z_step, y_step):
        return (z_hi + z_step) % 2 * 4 + (y + y_step) % 4

    top, bottom = matrix[:half], matrix[half:]
    other_z = over_row(matrix, 1, 0, 0)
    x_near = near(matrix, x_shift)
    y_near = near(matrix, y_shift)
    top, bottom, matrix_b, other_z, x_near, y_near = after((top, bottom, matrix, other_z, x_near, y_near))
    top_z = z_swap(top)
    x_far = far(*x_near, x_shift)
    y_far = far(*y_near, y_shift)
    swapped = {}
    swapped["own"] = core_swap(matrix_b)
    swapped["near"] = [core_swap(v) for v in y_near]
    bottom, top_z, x_far, y_far, other_z = after((bottom, top_z, x_far, y_far, other_z))
    w1, w2 = other_z[:half], other_z[half:]
    wm1, wp2 = y_shift(w1, 1), y_shift(w2, -1)
    bottom_z = z_swap(bottom)
    top_z_near = near(top_z, x_shift)
    bottom_z, top_z_near, wm1, wp2, w1, w2 = after((bottom_z, top_z_near, wm1, wp2, w1, w2))
    wm2, wp1 = y_shift(w2, 1), y_shift(w1, -1)
    bottom_z_near = near(bottom_z, x_shift)
    cross_top = x_shift(top_z_near[0], 1)
    wm1, wp2, wm2, wp1, bottom_z_near, y_far, other_z = after(
        (wm1, wp2, wm2, wp1, bottom_z_near, y_far, other_z)
    )
    z_far = y_shift(wm1, 1), y_shift(wp2, -1)
    cross_bottom = x_shift(bottom_z_near[1], -1)
    swapped["z"] = core_swap(other_z)
    swapped["far"] = [core_swap(v) for v in y_far]
    z_near = [(wm1, wm2), (wp1, wp2)]
    swapped["z near"] = [[core_swap(v) for v in pair] for pair in z_near]
    z_far, cross_bottom = after((z_far, cross_bottom))
    z_cross = cross_top, cross_bottom
    swapped["z far"] = [core_swap(v) for v in z_far]

    def in_two(pair):
        return [(pair[0], 0), (pair[1], half)]

    pieces = [
        (0, 0, [(matrix, 0)], [(swapped["own"], 0)]),
        (0, -1, [(y_near[0], 0)], [(swapped["near"][0], 0)]),
        (0, 1, [(y_near[1], 0)], [(swapped["near"][1], 0)]),
        (0, 2, [(y_far[0], 0), (y_far[1], half)], [(swapped["far"][0], 0), (swapped["far"][1], half)]),
        (1, 0, [(other_z, 0)], [(swapped["z"], 0)]),
        (1, -1, in_two(z_near[0]), in_two(swapped["z near"][0])),
        (1, 1, in_two(z_near[1]), in_two(swapped["z near"][1])),
        (1, 2, [(z_far[0], 0), (z_far[1], half)], [(swapped["z far"][0], 0), (swapped["z far"][1], half)]),
    ]
    chunks = [(row_chunk(z_step, y_step), mine, others) for z_step, y_step, mine, others in pieces]

    def strip(z_step, own, near_two, far_parts):
        parts = [
            (value, col_chunk(z_step, step), 0, 0, half) for value, step in zip((own, *near_two), (0, -1, 1))
        ]
        count = half // len(far_parts)
        return parts + [
            (value, col_chunk(z_step, 2), 0, index * count, count) for index, value in enumerate(far_parts)
        ]

    factor = 0.5 / (matrix.shape[1] * lax.axis_size("col"))
    kind = matrix.dtype
    def both(z_step, first, second):
        parts = []
        for below, (own, near_two, far_two) in ((0, first), (half, second)):
            for array, chunk, source, row_at, count in strip(z_step, own, near_two, far_two):
                parts.append((array, chunk, source, row_at + below, count))
        return parts

    lefts = [(value, col_chunk(0, step), 0, 0, rows) for value, step in ((matrix, 0), (x_near[0], -1), (x_near[1], 1))]
    lefts += [(value, col_chunk(0, 2), 0, index * half, half) for index, value in enumerate(x_far)]
    for below, own, two, cross in ((0, top_z, top_z_near, z_cross[0]), (half, bottom_z, bottom_z_near, z_cross[1])):
        for value, step in ((own, 0), (two[0], -1), (two[1], 1), (cross, 2)):
            lefts.append((value, col_chunk(1, step), 0, below, half))
    h1, h2 = product(lefts, chunks, core, [half, half], factor, kind, "square")
    h2_z, h1_z = z_swap(h2), z_swap(h1)
    h1_near, h2_near = near(h1, x_shift), near(h2, x_shift)
    h1_near, h2_near, h1_z, h2_z, h1, h2 = after((h1_near, h2_near, h1_z, h2_z, h1, h2))
    h1_far, h2_far = x_shift(h1_near[0], 1), x_shift(h2_near[1], -1)
    h1_z_near = [z_swap(v) for v in h1_near]
    h1_far, h2_far, h2_z = after((h1_far, h2_far, h2_z))
    h2_z_near = near(h2_z, x_shift)
    h1_z_far = z_swap(h1_far)
    lefts = both(0, (h1, h1_near, [h1_far]), (h2, h2_near, [h2_far]))
    (total,) = product(lefts, chunks, core, [rows], 1.0, jnp.float32, "step_first", z_lo)
    h2_z_near, h1_z_near, total = after((h2_z_near, h1_z_near, total))
    h2_z_far = far(*h2_z_near, x_shift)
    h1_z_far = [h1_z_far]
    late = (h1_z, h1_z_near, h1_z_far, h2_z, h2_z_near, h2_z_far)
    h1_z, h1_z_near, h1_z_far, h2_z, h2_z_near, h2_z_far = after(late, total)
    lefts = both(1, (h1_z, h1_z_near, h1_z_far), (h2_z, h2_z_near, h2_z_far))
    (out,) = product(lefts, chunks, core, [rows], 1.0, jnp.float32, "step_last", 1 - z_lo, total, matrix)
    return out


def solution(mesh):
    placed = (P("row", "col", None), P("row", "col"), P("row", "col"), P("row", "col"))
    return jax.shard_map(
        local, mesh=mesh, in_specs=placed, out_specs=P("row", "col"), check_vma=False
    )
```

```python
import functools

import jax
import jax.numpy as jnp
from jax import lax
from jax.experimental import pallas as pl
from jax.experimental.pallas import tpu as pltpu
from jax.sharding import PartitionSpec as P

BLOCK = 128
BR = 4
BC = 8
CAP = 2
META = 16
NONE = 64


def pack_kernel(atom, column, count, blocks, send, seen, place):
    groups = send.shape[0]
    slots = blocks.shape[0]
    send[...] = jnp.zeros_like(send)
    for group in range(groups):
        seen[group] = 0
        for turn in range(CAP):
            place[group * CAP + turn] = NONE

    @pl.loop(0, slots)
    def _(slot):
        @pl.when(slot < count[0, 0])
        def _():
            group = atom[slot] // BR
            turn = jnp.minimum(seen[group], CAP - 1)
            seen[group] = turn + 1
            place[group * CAP + turn] = atom[slot] % BR * BC + column[slot]
            start = pl.multiple_of(turn * BLOCK, BLOCK)
            send[group, pl.ds(start, BLOCK), :] = blocks[slot]

    row = lax.broadcasted_iota(jnp.int32, (META, BLOCK), 0)
    for group in range(groups):
        value = jnp.where(row == 0, place[group * CAP], place[group * CAP + 1])
        send[group, CAP * BLOCK :, :] = value.astype(jnp.float32).astype(send.dtype)


def unpack_kernel(received, tile, place_vector, place, sem):
    owners = received.shape[0]
    tile[...] = jnp.zeros_like(tile)
    lane = lax.broadcasted_iota(jnp.int32, (META, BLOCK), 1)
    places = jnp.full((META, BLOCK), NONE, jnp.int32)
    for owner in range(owners):
        value = received[owner, CAP * BLOCK :, :].astype(jnp.float32).astype(jnp.int32)
        places = jnp.where(lane == owner, value, places)
    place_vector[...] = places
    copy = pltpu.make_async_copy(place_vector, place, sem)
    copy.start()
    copy.wait()

    @pl.loop(0, owners)
    def _(owner):
        for turn in range(CAP):
            at = place[turn, owner]

            @pl.when(at < BR * BC)
            def _():
                top = pl.multiple_of(at // BC * BLOCK, BLOCK)
                left = pl.multiple_of(at % BC * BLOCK, BLOCK)
                block = received[owner, turn * BLOCK : (turn + 1) * BLOCK, :]
                tile[pl.ds(top, BLOCK), pl.ds(left, BLOCK)] = block


def local_tile(blocks, block_atom, block_col, block_count):
    owners = lax.axis_size("row")
    vmem = pl.BlockSpec(memory_space=pltpu.VMEM)
    smem = pl.BlockSpec(memory_space=pltpu.SMEM)
    send = pl.pallas_call(
        pack_kernel,
        out_shape=jax.ShapeDtypeStruct((owners, CAP * BLOCK + META, BLOCK), blocks.dtype),
        in_specs=[smem, smem, smem, vmem],
        out_specs=vmem,
        scratch_shapes=[pltpu.SMEM((owners,), jnp.int32), pltpu.SMEM((owners * CAP,), jnp.int32)],
        compiler_params=pltpu.CompilerParams(vmem_limit_bytes=16 << 20),
        name="pack",
    )(block_atom[:, 0], block_col[:, 0], block_count, blocks)
    received = lax.all_to_all(send, "row", 0, 0, tiled=True)
    return pl.pallas_call(
        unpack_kernel,
        out_shape=jax.ShapeDtypeStruct((BR * BLOCK, BC * BLOCK), blocks.dtype),
        in_specs=[vmem],
        out_specs=vmem,
        scratch_shapes=[
            pltpu.VMEM((META, BLOCK), jnp.int32),
            pltpu.SMEM((META, BLOCK), jnp.int32),
            pltpu.SemaphoreType.DMA,
        ],
        compiler_params=pltpu.CompilerParams(vmem_limit_bytes=16 << 20),
        name="unpack",
    )(received)


def product_kernel(factor, left_parts, right_parts, part, first_total, has_base, n_out, left_at, right_at, core, want, *refs):
    lefts, refs = refs[: len(left_parts)], refs[len(left_parts) :]
    n_right = sum(len(pieces) for chunk in right_parts for pieces in chunk)
    rights, refs = list(refs[:n_right]), refs[n_right:]
    if first_total:
        total_in, refs = refs[0], refs[1:]
    if has_base:
        base, refs = refs[0], refs[1:]
    outs, (held, staged, total, total_held, base_held, left_sems, right_sems, extra_sems) = refs[:n_out], refs[n_out:]
    places, (slots, depth, _) = held.shape[0], staged.shape
    copies = []
    for index, (left, (source, first, count)) in enumerate(zip(lefts, left_parts)):
        place = left_at[index] % places
        target = held.at[place, pl.ds(first, count)]
        copies.append(pltpu.make_async_copy(left.at[pl.ds(source, count)], target, left_sems.at[place]))
    loads = []
    for index, chunk in enumerate(right_parts):
        load = []
        for step, pieces in enumerate(chunk):
            down = (core[0] + step) % 2 * (depth // 2)
            for first, count in pieces:
                target = staged.at[index % slots, pl.ds(pl.multiple_of(down + first, count), count)]
                sem = right_sems.at[index % slots]
                load.append(pltpu.make_async_copy(rights.pop(0), target, sem))
        loads.append(load)

    def when_wanted(index, act):
        if part:
            pl.when(right_at[index] // places == want[0])(act)
        else:
            act()

    def start(index):
        for load in loads[index]:
            load.start()
        for at, copy in enumerate(copies):
            pl.when(left_at[at] == right_at[index])(copy.start)

    for index in range(slots - 1):
        when_wanted(index, functools.partial(start, index))
    total[...] = jnp.zeros_like(total)
    if first_total:
        total_copy = pltpu.make_async_copy(total_in, total_held, extra_sems.at[0])
        total_copy.start()
    if has_base:
        base_copy = pltpu.make_async_copy(base, base_held, extra_sems.at[1])
        base_copy.start()

    @pl.loop(0, len(loads))
    def _(index):
        for ahead in range(slots - 1, len(loads)):

            @pl.when(index == ahead - slots + 1)
            def _():
                when_wanted(ahead, functools.partial(start, ahead))

        def add():
            place, slot = right_at[index] % places, index % slots
            pltpu.make_async_copy(held.at[place], held.at[place], left_sems.at[place]).wait()
            pltpu.make_async_copy(staged.at[slot], staged.at[slot], right_sems.at[slot]).wait()
            total[...] += jnp.dot(held[place], staged[slot], preferred_element_type=jnp.float32)

        when_wanted(index, add)

    if first_total:
        total_copy.wait()
    if has_base:
        base_copy.wait()
    first = 0
    for out in outs:
        count = out.shape[0]
        value = total[first : first + count, :]
        if first_total:
            value += total_held[first : first + count, :]
        value *= factor
        if has_base:
            value = 1.5 * base_held[first : first + count, :].astype(jnp.float32) - value
        out[...] = value.astype(out.dtype)
        first += count


def product(lefts, rights, core, outs, factor, dtype, name, part=None, first_total=None, base=None):
    width = lefts[0][0].shape[1]
    kind = lefts[0][0].dtype
    left_parts = [(source, first, count) for _, _, source, first, count in lefts]
    right_parts = [
        [[(first, array.shape[0]) for array, first in pieces] for pieces in chunk[1:]] for chunk in rights
    ]
    left_at = jnp.stack([chunk for _, chunk, *_ in lefts]).astype(jnp.int32)
    right_at = jnp.stack([chunk for chunk, *_ in rights]).astype(jnp.int32)
    want = jnp.asarray(0 if part is None else part, jnp.int32)[None]
    smem = pl.BlockSpec(memory_space=pltpu.SMEM)
    vmem = pl.BlockSpec(memory_space=pltpu.VMEM)
    hbm = pl.BlockSpec(memory_space=pltpu.HBM)
    arrays = [left for left, *_ in lefts]
    arrays += [array for chunk in rights for pieces in chunk[1:] for array, _ in pieces]
    extra = [value for value in (first_total, base) if value is not None]
    count = len(rights) if part is None else len(rights) // 2
    rows = sum(outs)
    slots = 3
    return pl.pallas_call(
        functools.partial(
            product_kernel,
            factor,
            left_parts,
            right_parts,
            part is not None,
            first_total is not None,
            base is not None,
            len(outs),
        ),
        out_shape=[jax.ShapeDtypeStruct((out, width), dtype) for out in outs],
        in_specs=[smem] * 4 + [hbm] * (len(arrays) + len(extra)),
        out_specs=[vmem] * len(outs),
        scratch_shapes=[
            pltpu.VMEM((count, rows, width), kind),
            pltpu.VMEM((slots, width, width), kind),
            pltpu.VMEM((rows, width), jnp.float32),
            pltpu.VMEM((rows, width), jnp.float32),
            pltpu.VMEM((rows, width), kind),
            pltpu.SemaphoreType.DMA((count,)),
            pltpu.SemaphoreType.DMA((slots,)),
            pltpu.SemaphoreType.DMA((2,)),
        ],
        compiler_params=pltpu.CompilerParams(vmem_limit_bytes=58 << 20),
        cost_estimate=pl.CostEstimate(
            flops=2 * rows * width * width * count, bytes_accessed=2 * width * count * (rows + width), transcendentals=0
        ),
        name=name,
    )(left_at, right_at, core.astype(jnp.int32)[None], want, *arrays, *extra)


def over_row(value, z_step, y_step, core_step):
    size = lax.axis_size("row")
    pairs = []
    for source in range(size):
        z, y, core = source // 8, source // 2 % 4, source % 2
        target = ((z + z_step) % 2 * 4 + (y + y_step) % 4) * 2 + (core + core_step) % 2
        pairs.append((source, target))
    return lax.ppermute(value, "row", pairs)


def over_col(value, z_step, x_step):
    size = lax.axis_size("col")
    pairs = []
    for source in range(size):
        z, x = source // 4, source % 4
        pairs.append((source, (z + z_step) % 2 * 4 + (x + x_step) % 4))
    return lax.ppermute(value, "col", pairs)


def x_shift(value, step):
    return over_col(value, 0, step)


def y_shift(value, step):
    return over_row(value, 0, step, 0)


def z_swap(value):
    return over_col(value, 1, 0)


def core_swap(value):
    return over_row(value, 0, 0, 1)


def after(values, *earlier):
    return lax.optimization_barrier((values, earlier))[0]


def near(value, shift):
    return shift(value, 1), shift(value, -1)


def far(below, above, shift):
    half = below.shape[0] // 2
    return shift(below[:half], 1), shift(above[half:], -1)


def local(blocks, block_atom, block_col, block_count):
    matrix = local_tile(blocks, block_atom, block_col, block_count)
    rows = matrix.shape[0]
    half = rows // 2
    quarter = half // 2
    row, col = lax.axis_index("row"), lax.axis_index("col")
    z_hi, y, core = row // 8, row // 2 % 4, row % 2
    z_lo, x = col // 4, col % 4

    def col_chunk(z_step, x_step):
        return (z_lo + z_step) % 2 * 4 + (x + x_step) % 4

    def row_chunk(z_step, y_step):
        return (z_hi + z_step) % 2 * 4 + (y + y_step) % 4

    top, bottom = matrix[:half], matrix[half:]
    other_z = over_row(matrix, 1, 0, 0)
    x_near = near(matrix, x_shift)
    y_near = near(matrix, y_shift)
    top, bottom, matrix_b, other_z, x_near, y_near = after((top, bottom, matrix, other_z, x_near, y_near))
    top_z = z_swap(top)
    x_far = far(*x_near, x_shift)
    y_far = far(*y_near, y_shift)
    swapped = {}
    swapped["own"] = core_swap(matrix_b)
    swapped["near"] = [core_swap(v) for v in y_near]
    bottom, top_z, x_far, y_far, other_z = after((bottom, top_z, x_far, y_far, other_z))
    w1, w2 = other_z[:half], other_z[half:]
    wm1, wp2 = y_shift(w1, 1), y_shift(w2, -1)
    bottom_z = z_swap(bottom)
    top_z_near = near(top_z, x_shift)
    bottom_z, top_z_near, wm1, wp2, w1, w2 = after((bottom_z, top_z_near, wm1, wp2, w1, w2))
    wm2, wp1 = y_shift(w2, 1), y_shift(w1, -1)
    bottom_z_near = near(bottom_z, x_shift)
    cross_top = x_shift(top_z_near[0], 1)
    wm1, wp2, wm2, wp1, bottom_z_near, y_far, other_z = after(
        (wm1, wp2, wm2, wp1, bottom_z_near, y_far, other_z)
    )
    z_far = y_shift(wm1, 1), y_shift(wp2, -1)
    cross_bottom = x_shift(bottom_z_near[1], -1)
    swapped["z"] = core_swap(other_z)
    swapped["far"] = [core_swap(v) for v in y_far]
    z_near = [(wm1, wm2), (wp1, wp2)]
    swapped["z near"] = [[core_swap(v) for v in pair] for pair in z_near]
    z_far, cross_bottom = after((z_far, cross_bottom))
    z_cross = cross_top, cross_bottom
    swapped["z far"] = [core_swap(v) for v in z_far]

    def in_two(pair):
        return [(pair[0], 0), (pair[1], half)]

    pieces = [
        (0, 0, [(matrix, 0)], [(swapped["own"], 0)]),
        (0, -1, [(y_near[0], 0)], [(swapped["near"][0], 0)]),
        (0, 1, [(y_near[1], 0)], [(swapped["near"][1], 0)]),
        (0, 2, [(y_far[0], 0), (y_far[1], half)], [(swapped["far"][0], 0), (swapped["far"][1], half)]),
        (1, 0, [(other_z, 0)], [(swapped["z"], 0)]),
        (1, -1, in_two(z_near[0]), in_two(swapped["z near"][0])),
        (1, 1, in_two(z_near[1]), in_two(swapped["z near"][1])),
        (1, 2, [(z_far[0], 0), (z_far[1], half)], [(swapped["z far"][0], 0), (swapped["z far"][1], half)]),
    ]
    chunks = [(row_chunk(z_step, y_step), mine, others) for z_step, y_step, mine, others in pieces]

    def strip(z_step, own, near_two, far_parts):
        parts = [
            (value, col_chunk(z_step, step), 0, 0, half) for value, step in zip((own, *near_two), (0, -1, 1))
        ]
        count = half // len(far_parts)
        return parts + [
            (value, col_chunk(z_step, 2), 0, index * count, count) for index, value in enumerate(far_parts)
        ]

    factor = 0.5 / (matrix.shape[1] * lax.axis_size("col"))
    kind = matrix.dtype
    def both(z_step, first, second):
        parts = []
        for below, (own, near_two, far_two) in ((0, first), (half, second)):
            for array, chunk, source, row_at, count in strip(z_step, own, near_two, far_two):
                parts.append((array, chunk, source, row_at + below, count))
        return parts

    lefts = [(value, col_chunk(0, step), 0, 0, rows) for value, step in ((matrix, 0), (x_near[0], -1), (x_near[1], 1))]
    lefts += [(value, col_chunk(0, 2), 0, index * half, half) for index, value in enumerate(x_far)]
    for below, own, two, cross in ((0, top_z, top_z_near, z_cross[0]), (half, bottom_z, bottom_z_near, z_cross[1])):
        for value, step in ((own, 0), (two[0], -1), (two[1], 1), (cross, 2)):
            lefts.append((value, col_chunk(1, step), 0, below, half))
    h1, h2 = product(lefts, chunks, core, [half, half], factor, kind, "square")
    h2_z, h1_z = z_swap(h2), z_swap(h1)
    h1_near, h2_near = near(h1, x_shift), near(h2, x_shift)
    h1_near, h2_near, h1, h2 = after((h1_near, h2_near, h1, h2))
    h1_far, h2_far = x_shift(h1_near[0], 1), x_shift(h2_near[1], -1)
    h1_z_near = [z_swap(v) for v in h1_near]
    h1_far, h2_far, h1_z, h2_z = after((h1_far, h2_far, h1_z, h2_z))
    h2_z_near = near(h2_z, x_shift)
    h1_z_far = z_swap(h1_far)
    lefts = both(0, (h1, h1_near, [h1_far]), (h2, h2_near, [h2_far]))
    (total,) = product(lefts, chunks, core, [rows], 1.0, jnp.float32, "step_first", z_lo)
    h2_z_near, h1_z_near, total = after((h2_z_near, h1_z_near, total))
    h2_z_far = far(*h2_z_near, x_shift)
    h1_z_far = [h1_z_far]
    late = (h1_z, h1_z_near, h1_z_far, h2_z, h2_z_near, h2_z_far)
    h1_z, h1_z_near, h1_z_far, h2_z, h2_z_near, h2_z_far = after(late, total)
    lefts = both(1, (h1_z, h1_z_near, h1_z_far), (h2_z, h2_z_near, h2_z_far))
    (out,) = product(lefts, chunks, core, [rows], 1.0, jnp.float32, "step_last", 1 - z_lo, total, matrix)
    return out


def solution(mesh):
    placed = (P("row", "col", None), P("row", "col"), P("row", "col"), P("row", "col"))
    return jax.shard_map(
        local, mesh=mesh, in_specs=placed, out_specs=P("row", "col"), check_vma=False
    )
```

```python
import functools

import jax
import jax.numpy as jnp
from jax import lax
from jax.experimental import pallas as pl
from jax.experimental.pallas import tpu as pltpu
from jax.sharding import PartitionSpec as P

BLOCK = 128
BR = 4
BC = 8
CAP = 2
META = 16
NONE = 64


def pack_kernel(atom, column, count, blocks, send, seen, place, sems):
    groups = send.shape[0]
    slots = blocks.shape[0]
    send[...] = jnp.zeros_like(send)
    for group in range(groups):
        seen[group] = 0
        for turn in range(CAP):
            place[group * CAP + turn] = NONE

    @pl.loop(0, slots)
    def _(slot):
        @pl.when(slot < count[0, 0])
        def _():
            group = atom[slot] // BR
            turn = jnp.minimum(seen[group], CAP - 1)
            seen[group] = turn + 1
            place[group * CAP + turn] = atom[slot] % BR * BC + column[slot]
            start = pl.multiple_of(turn * BLOCK, BLOCK)
            target = send.at[group, pl.ds(start, BLOCK)]
            pltpu.make_async_copy(blocks.at[slot], target, sems.at[slot]).start()

    row = lax.broadcasted_iota(jnp.int32, (META, BLOCK), 0)
    for group in range(groups):
        value = jnp.where(row == 0, place[group * CAP], place[group * CAP + 1])
        send[group, CAP * BLOCK :, :] = value.astype(jnp.float32).astype(send.dtype)

    @pl.loop(0, slots)
    def _(slot):
        @pl.when(slot < count[0, 0])
        def _():
            pltpu.make_async_copy(blocks.at[slot], send.at[0, pl.ds(0, BLOCK)], sems.at[slot]).wait()


def unpack_kernel(received, tile, place_vector, place, sem):
    owners = received.shape[0]
    tile[...] = jnp.zeros_like(tile)
    lane = lax.broadcasted_iota(jnp.int32, (META, BLOCK), 1)
    places = jnp.full((META, BLOCK), NONE, jnp.int32)
    for owner in range(owners):
        value = received[owner, CAP * BLOCK :, :].astype(jnp.float32).astype(jnp.int32)
        places = jnp.where(lane == owner, value, places)
    place_vector[...] = places
    copy = pltpu.make_async_copy(place_vector, place, sem)
    copy.start()
    copy.wait()

    @pl.loop(0, owners)
    def _(owner):
        for turn in range(CAP):
            at = place[turn, owner]

            @pl.when(at < BR * BC)
            def _():
                top = pl.multiple_of(at // BC * BLOCK, BLOCK)
                left = pl.multiple_of(at % BC * BLOCK, BLOCK)
                block = received[owner, turn * BLOCK : (turn + 1) * BLOCK, :]
                tile[pl.ds(top, BLOCK), pl.ds(left, BLOCK)] = block


def local_tile(blocks, block_atom, block_col, block_count):
    owners = lax.axis_size("row")
    vmem = pl.BlockSpec(memory_space=pltpu.VMEM)
    smem = pl.BlockSpec(memory_space=pltpu.SMEM)
    send = pl.pallas_call(
        pack_kernel,
        out_shape=jax.ShapeDtypeStruct((owners, CAP * BLOCK + META, BLOCK), blocks.dtype),
        in_specs=[smem, smem, smem, pl.BlockSpec(memory_space=pltpu.HBM)],
        out_specs=vmem,
        scratch_shapes=[pltpu.SMEM((owners,), jnp.int32), pltpu.SMEM((owners * CAP,), jnp.int32), pltpu.SemaphoreType.DMA((blocks.shape[0],))],
        compiler_params=pltpu.CompilerParams(vmem_limit_bytes=58 << 20),
        name="pack",
    )(block_atom[:, 0], block_col[:, 0], block_count, blocks)
    received = lax.all_to_all(send, "row", 0, 0, tiled=True)
    return pl.pallas_call(
        unpack_kernel,
        out_shape=jax.ShapeDtypeStruct((BR * BLOCK, BC * BLOCK), blocks.dtype),
        in_specs=[vmem],
        out_specs=vmem,
        scratch_shapes=[
            pltpu.VMEM((META, BLOCK), jnp.int32),
            pltpu.SMEM((META, BLOCK), jnp.int32),
            pltpu.SemaphoreType.DMA,
        ],
        compiler_params=pltpu.CompilerParams(vmem_limit_bytes=16 << 20),
        name="unpack",
    )(received)


def product_kernel(factor, left_parts, right_parts, part, first_total, has_base, n_out, left_at, right_at, core, want, *refs):
    lefts, refs = refs[: len(left_parts)], refs[len(left_parts) :]
    n_right = sum(len(pieces) for chunk in right_parts for pieces in chunk)
    rights, refs = list(refs[:n_right]), refs[n_right:]
    if first_total:
        total_in, refs = refs[0], refs[1:]
    if has_base:
        base, refs = refs[0], refs[1:]
    outs, (held, staged, total, total_held, base_held, left_sems, right_sems, extra_sems) = refs[:n_out], refs[n_out:]
    places, (slots, depth, _) = held.shape[0], staged.shape
    copies = []
    for index, (left, (source, first, count)) in enumerate(zip(lefts, left_parts)):
        place = left_at[index] % places
        target = held.at[place, pl.ds(first, count)]
        copies.append(pltpu.make_async_copy(left.at[pl.ds(source, count)], target, left_sems.at[place]))
    loads = []
    for index, chunk in enumerate(right_parts):
        load = []
        for step, pieces in enumerate(chunk):
            down = (core[0] + step) % 2 * (depth // 2)
            for first, count in pieces:
                target = staged.at[index % slots, pl.ds(pl.multiple_of(down + first, count), count)]
                sem = right_sems.at[index % slots]
                load.append(pltpu.make_async_copy(rights.pop(0), target, sem))
        loads.append(load)

    def when_wanted(index, act):
        if part:
            pl.when(right_at[index] // places == want[0])(act)
        else:
            act()

    def start(index):
        for load in loads[index]:
            load.start()
        for at, copy in enumerate(copies):
            pl.when(left_at[at] == right_at[index])(copy.start)

    for index in range(slots - 1):
        when_wanted(index, functools.partial(start, index))
    total[...] = jnp.zeros_like(total)
    if first_total:
        total_copy = pltpu.make_async_copy(total_in, total_held, extra_sems.at[0])
        total_copy.start()
    if has_base:
        base_copy = pltpu.make_async_copy(base, base_held, extra_sems.at[1])
        base_copy.start()

    @pl.loop(0, len(loads))
    def _(index):
        for ahead in range(slots - 1, len(loads)):

            @pl.when(index == ahead - slots + 1)
            def _():
                when_wanted(ahead, functools.partial(start, ahead))

        def add():
            place, slot = right_at[index] % places, index % slots
            pltpu.make_async_copy(held.at[place], held.at[place], left_sems.at[place]).wait()
            pltpu.make_async_copy(staged.at[slot], staged.at[slot], right_sems.at[slot]).wait()
            total[...] += jnp.dot(held[place], staged[slot], preferred_element_type=jnp.float32)

        when_wanted(index, add)

    if first_total:
        total_copy.wait()
    if has_base:
        base_copy.wait()
    first = 0
    for out in outs:
        count = out.shape[0]
        value = total[first : first + count, :]
        if first_total:
            value += total_held[first : first + count, :]
        value *= factor
        if has_base:
            value = 1.5 * base_held[first : first + count, :].astype(jnp.float32) - value
        out[...] = value.astype(out.dtype)
        first += count


def product(lefts, rights, core, outs, factor, dtype, name, part=None, first_total=None, base=None):
    width = lefts[0][0].shape[1]
    kind = lefts[0][0].dtype
    left_parts = [(source, first, count) for _, _, source, first, count in lefts]
    right_parts = [
        [[(first, array.shape[0]) for array, first in pieces] for pieces in chunk[1:]] for chunk in rights
    ]
    left_at = jnp.stack([chunk for _, chunk, *_ in lefts]).astype(jnp.int32)
    right_at = jnp.stack([chunk for chunk, *_ in rights]).astype(jnp.int32)
    want = jnp.asarray(0 if part is None else part, jnp.int32)[None]
    smem = pl.BlockSpec(memory_space=pltpu.SMEM)
    vmem = pl.BlockSpec(memory_space=pltpu.VMEM)
    hbm = pl.BlockSpec(memory_space=pltpu.HBM)
    arrays = [left for left, *_ in lefts]
    arrays += [array for chunk in rights for pieces in chunk[1:] for array, _ in pieces]
    extra = [value for value in (first_total, base) if value is not None]
    count = len(rights) if part is None else len(rights) // 2
    rows = sum(outs)
    slots = 3
    return pl.pallas_call(
        functools.partial(
            product_kernel,
            factor,
            left_parts,
            right_parts,
            part is not None,
            first_total is not None,
            base is not None,
            len(outs),
        ),
        out_shape=[jax.ShapeDtypeStruct((out, width), dtype) for out in outs],
        in_specs=[smem] * 4 + [hbm] * (len(arrays) + len(extra)),
        out_specs=[vmem] * len(outs),
        scratch_shapes=[
            pltpu.VMEM((count, rows, width), kind),
            pltpu.VMEM((slots, width, width), kind),
            pltpu.VMEM((rows, width), jnp.float32),
            pltpu.VMEM((rows, width), jnp.float32),
            pltpu.VMEM((rows, width), kind),
            pltpu.SemaphoreType.DMA((count,)),
            pltpu.SemaphoreType.DMA((slots,)),
            pltpu.SemaphoreType.DMA((2,)),
        ],
        compiler_params=pltpu.CompilerParams(vmem_limit_bytes=58 << 20),
        cost_estimate=pl.CostEstimate(
            flops=2 * rows * width * width * count, bytes_accessed=2 * width * count * (rows + width), transcendentals=0
        ),
        name=name,
    )(left_at, right_at, core.astype(jnp.int32)[None], want, *arrays, *extra)


def over_row(value, z_step, y_step, core_step):
    size = lax.axis_size("row")
    pairs = []
    for source in range(size):
        z, y, core = source // 8, source // 2 % 4, source % 2
        target = ((z + z_step) % 2 * 4 + (y + y_step) % 4) * 2 + (core + core_step) % 2
        pairs.append((source, target))
    return lax.ppermute(value, "row", pairs)


def over_col(value, z_step, x_step):
    size = lax.axis_size("col")
    pairs = []
    for source in range(size):
        z, x = source // 4, source % 4
        pairs.append((source, (z + z_step) % 2 * 4 + (x + x_step) % 4))
    return lax.ppermute(value, "col", pairs)


def x_shift(value, step):
    return over_col(value, 0, step)


def y_shift(value, step):
    return over_row(value, 0, step, 0)


def z_swap(value):
    return over_col(value, 1, 0)


def core_swap(value):
    return over_row(value, 0, 0, 1)


def after(values, *earlier):
    return lax.optimization_barrier((values, earlier))[0]


def near(value, shift):
    return shift(value, 1), shift(value, -1)


def far(below, above, shift):
    half = below.shape[0] // 2
    return shift(below[:half], 1), shift(above[half:], -1)


def local(blocks, block_atom, block_col, block_count):
    matrix = local_tile(blocks, block_atom, block_col, block_count)
    rows = matrix.shape[0]
    half = rows // 2
    quarter = half // 2
    row, col = lax.axis_index("row"), lax.axis_index("col")
    z_hi, y, core = row // 8, row // 2 % 4, row % 2
    z_lo, x = col // 4, col % 4

    def col_chunk(z_step, x_step):
        return (z_lo + z_step) % 2 * 4 + (x + x_step) % 4

    def row_chunk(z_step, y_step):
        return (z_hi + z_step) % 2 * 4 + (y + y_step) % 4

    top, bottom = matrix[:half], matrix[half:]
    other_z = over_row(matrix, 1, 0, 0)
    x_near = near(matrix, x_shift)
    y_near = near(matrix, y_shift)
    top, bottom, matrix_b, other_z, x_near, y_near = after((top, bottom, matrix, other_z, x_near, y_near))
    top_z = z_swap(top)
    x_far = far(*x_near, x_shift)
    y_far = far(*y_near, y_shift)
    swapped = {}
    swapped["own"] = core_swap(matrix_b)
    swapped["near"] = [core_swap(v) for v in y_near]
    bottom, top_z, x_far, y_far, other_z = after((bottom, top_z, x_far, y_far, other_z))
    w1, w2 = other_z[:half], other_z[half:]
    wm1, wp2 = y_shift(w1, 1), y_shift(w2, -1)
    bottom_z = z_swap(bottom)
    top_z_near = near(top_z, x_shift)
    bottom_z, top_z_near, wm1, wp2, w1, w2 = after((bottom_z, top_z_near, wm1, wp2, w1, w2))
    wm2, wp1 = y_shift(w2, 1), y_shift(w1, -1)
    bottom_z_near = near(bottom_z, x_shift)
    cross_top = x_shift(top_z_near[0], 1)
    wm1, wp2, wm2, wp1, bottom_z_near, y_far, other_z = after(
        (wm1, wp2, wm2, wp1, bottom_z_near, y_far, other_z)
    )
    z_far = y_shift(wm1, 1), y_shift(wp2, -1)
    cross_bottom = x_shift(bottom_z_near[1], -1)
    swapped["z"] = core_swap(other_z)
    swapped["far"] = [core_swap(v) for v in y_far]
    z_near = [(wm1, wm2), (wp1, wp2)]
    swapped["z near"] = [[core_swap(v) for v in pair] for pair in z_near]
    z_far, cross_bottom = after((z_far, cross_bottom))
    z_cross = cross_top, cross_bottom
    swapped["z far"] = [core_swap(v) for v in z_far]

    def in_two(pair):
        return [(pair[0], 0), (pair[1], half)]

    pieces = [
        (0, 0, [(matrix, 0)], [(swapped["own"], 0)]),
        (0, -1, [(y_near[0], 0)], [(swapped["near"][0], 0)]),
        (0, 1, [(y_near[1], 0)], [(swapped["near"][1], 0)]),
        (0, 2, [(y_far[0], 0), (y_far[1], half)], [(swapped["far"][0], 0), (swapped["far"][1], half)]),
        (1, 0, [(other_z, 0)], [(swapped["z"], 0)]),
        (1, -1, in_two(z_near[0]), in_two(swapped["z near"][0])),
        (1, 1, in_two(z_near[1]), in_two(swapped["z near"][1])),
        (1, 2, [(z_far[0], 0), (z_far[1], half)], [(swapped["z far"][0], 0), (swapped["z far"][1], half)]),
    ]
    chunks = [(row_chunk(z_step, y_step), mine, others) for z_step, y_step, mine, others in pieces]

    def strip(z_step, own, near_two, far_parts):
        parts = [
            (value, col_chunk(z_step, step), 0, 0, half) for value, step in zip((own, *near_two), (0, -1, 1))
        ]
        count = half // len(far_parts)
        return parts + [
            (value, col_chunk(z_step, 2), 0, index * count, count) for index, value in enumerate(far_parts)
        ]

    factor = 0.5 / (matrix.shape[1] * lax.axis_size("col"))
    kind = matrix.dtype
    def both(z_step, first, second):
        parts = []
        for below, (own, near_two, far_two) in ((0, first), (half, second)):
            for array, chunk, source, row_at, count in strip(z_step, own, near_two, far_two):
                parts.append((array, chunk, source, row_at + below, count))
        return parts

    lefts = [(value, col_chunk(0, step), 0, 0, rows) for value, step in ((matrix, 0), (x_near[0], -1), (x_near[1], 1))]
    lefts += [(value, col_chunk(0, 2), 0, index * half, half) for index, value in enumerate(x_far)]
    for below, own, two, cross in ((0, top_z, top_z_near, z_cross[0]), (half, bottom_z, bottom_z_near, z_cross[1])):
        for value, step in ((own, 0), (two[0], -1), (two[1], 1), (cross, 2)):
            lefts.append((value, col_chunk(1, step), 0, below, half))
    h1, h2 = product(lefts, chunks, core, [half, half], factor, kind, "square")
    h2_z, h1_z = z_swap(h2), z_swap(h1)
    h1_near, h2_near = near(h1, x_shift), near(h2, x_shift)
    h1_near, h2_near, h1, h2 = after((h1_near, h2_near, h1, h2))
    h1_far, h2_far = x_shift(h1_near[0], 1), x_shift(h2_near[1], -1)
    h1_z_near = [z_swap(v) for v in h1_near]
    h1_far, h2_far, h1_z, h2_z = after((h1_far, h2_far, h1_z, h2_z))
    h2_z_near = near(h2_z, x_shift)
    h1_z_far = z_swap(h1_far)
    lefts = both(0, (h1, h1_near, [h1_far]), (h2, h2_near, [h2_far]))
    (total,) = product(lefts, chunks, core, [rows], 1.0, jnp.float32, "step_first", z_lo)
    h2_z_near, h1_z_near, total = after((h2_z_near, h1_z_near, total))
    h2_z_far = far(*h2_z_near, x_shift)
    h1_z_far = [h1_z_far]
    late = (h1_z, h1_z_near, h1_z_far, h2_z, h2_z_near, h2_z_far)
    h1_z, h1_z_near, h1_z_far, h2_z, h2_z_near, h2_z_far = after(late, total)
    lefts = both(1, (h1_z, h1_z_near, h1_z_far), (h2_z, h2_z_near, h2_z_far))
    (out,) = product(lefts, chunks, core, [rows], 1.0, jnp.float32, "step_last", 1 - z_lo, total, matrix)
    return out


def solution(mesh):
    placed = (P("row", "col", None), P("row", "col"), P("row", "col"), P("row", "col"))
    return jax.shard_map(
        local, mesh=mesh, in_specs=placed, out_specs=P("row", "col"), check_vma=False
    )
```
